256 devices in a mesh: vert: 64 (over y, x, z_lo), af: 4 (over z_hi, core).
Axes of the slice: x: 4, y: 4, z: 8 (z_hi: 2, z_lo: 4; z = z_hi * 4 + z_lo), core: 2. Of those that a mesh axis runs over, the one named last changes fastest.
Arguments:
- features: bfloat16 [256, 262144], P('af', 'vert'), may hold values from -6 to 6
- cotangent: bfloat16 [256, 262144], P('af', 'vert'), may hold values from -6 to 6
- w_self: bfloat16 [256, 256], replicated, may hold values from -0.25 to 0.25
- w_neigh: bfloat16 [256, 256], replicated, may hold values from -0.25 to 0.25
- send_index: int32 [64, 64, 64], P('vert'), may hold values from 128 to 4095
- send_count: int32 [64, 64], P('vert'), may hold values from 0 to 64
- tile_index: int32 [2048, 8], P('vert'), may hold values from 0 to 127
- tile_count: int32 [2048], P('vert'), may hold values from 1 to 8
- tile_weight: bfloat16 [2048, 8, 128, 128], P('vert'), may hold values from -0.25 to 0.25
Outputs:
- output: bfloat16 [256, 262144], P('af', 'vert')
- grad_x: float32 [256, 262144], P('af', 'vert')
- grad_w_self: float32 [256, 256], P('af')
- grad_w_neigh: float32 [256, 256], P('af')
The draws below stay inside these ranges and needn't reach their ends.
Inputs may be any that keep to these rules, and one draw needn't show every extreme that they name: `tile_index`: tile numbers into an owner's source columns: its own vertices, then incoming boundary rows in sender order, then all hubs in owner order. `send_index`: boundary rows are never hubs.
All inputs are finite; a program needn't handle non-finite values.
Results may differ from the reference program's by a relative error of at most 0.0054.
Values may be sent and summed in bfloat16 or wider, within the bound.
No kernel may reach another device: no remote copies, remote signals or barrier semaphores. Data moves between devices by JAX's collectives and lax.ppermute only.
A program may use at most 128 MiB of HBM per device.

```python
import math
import jax
import jax.numpy as jnp
from jax import lax

F = 256
FO = 256
TILE = 128
TPB = 8
HUB_DEV = 128
NLOC = 4096
SLOTS = 64
NT = 32
BLOCKS = 2048
NODES = 262144
HUBS = 8192
SRC_TILES = 128
N_VERT = 64


def draw_send_count(key, part):
    key = jax.random.fold_in(key, 11)
    first, second = jax.random.split(key)
    counts = jax.random.randint(first, (N_VERT, N_VERT), 0, SLOTS + 1).astype(jnp.int32)
    spot = jax.random.randint(second, (), 0, N_VERT * N_VERT)
    flat = jnp.where(jnp.arange(N_VERT * N_VERT) == spot, SLOTS, counts.reshape(-1))
    return flat.reshape(N_VERT, N_VERT).astype(jnp.int32)


def draw_tile_count(key, part):
    key = jax.random.fold_in(key, 23)
    first, second, third, fourth = jax.random.split(key, 4)
    extra = jax.random.randint(first, (N_VERT, 1), 0, TPB // 2 + 1)
    base = jax.random.randint(second, (N_VERT, NT), 1, TPB + 1)
    counts = jnp.minimum(base + extra, TPB).reshape(-1)
    top_spot = jax.random.randint(third, (), 0, N_VERT * NT)
    low_spot = jax.random.randint(fourth, (), 0, N_VERT * NT)
    places = jnp.arange(N_VERT * NT)
    counts = jnp.where(places == low_spot, 1, counts)
    counts = jnp.where(places == top_spot, TPB, counts)
    return counts.astype(jnp.int32)


def set_ends(entries, stream_key, least, high):
    longest = entries.shape.index(max(entries.shape))
    spots = []
    for shift in (0, 1):
        where = [jax.random.randint(jax.random.fold_in(stream_key, axis), (), 0, length) for axis, length in enumerate(entries.shape)]
        where[longest] = (where[longest] + shift) % entries.shape[longest]
        spots.append(tuple(where))
    return entries.at[spots[0]].set(least).at[spots[1]].set(high)


def block_scale(key, shape, shards, least, top_value):
    def one(axis_at, parts):
        draws = jax.random.uniform(jax.random.fold_in(jax.random.fold_in(key, 6), axis_at), (parts,), jnp.float32, least / len(shards), top_value / len(shards))
        return jnp.repeat(jnp.exp(draws), shape[axis_at] // parts).reshape((-1,) + (1,) * (len(shape) - axis_at - 1))

    factor_of = one(*shards[0])
    for cut in shards[1:]:
        factor_of = factor_of * one(*cut)
    return factor_of


def scatter_about(stream_key, shape, deviation, bound, shards=(), kind=jnp.bfloat16):
    gain = block_scale(stream_key, shape, shards, -0.22, 0.18) if shards else 1.0
    values = jax.random.normal(stream_key, shape, jnp.float32) * deviation * gain
    return jnp.minimum(jnp.maximum(values, -bound), bound).astype(kind)


def setup_inputs(seed: int = 0) -> dict:
    streams_of = jax.random.split(jax.random.key(seed), 10)
    return {
        "features": scatter_about(streams_of[0], (F, NODES), 1.0, 6.0, ((0, 4), (1, 64))),
        "cotangent": scatter_about(streams_of[1], (FO, NODES), 1.0, 6.0, ((0, 4), (1, 64))),
        "w_self": scatter_about(streams_of[2], (F, FO), (2 * F) ** -0.5, 0.25),
        "w_neigh": scatter_about(streams_of[3], (F, FO), (2 * F) ** -0.5, 0.25),
        "send_index": set_ends(jax.random.randint(streams_of[4], (N_VERT, N_VERT, SLOTS), HUB_DEV, NLOC), jax.random.fold_in(streams_of[4], 1), HUB_DEV, NLOC - 1).astype(jnp.int32),
        "send_count": draw_send_count(jax.random.fold_in(streams_of[9], 71), 0),
        "tile_index": set_ends(jax.random.randint(streams_of[6], (BLOCKS, TPB), 0, SRC_TILES), jax.random.fold_in(streams_of[6], 1), 0, SRC_TILES - 1).astype(jnp.int32),
        "tile_count": draw_tile_count(jax.random.fold_in(streams_of[9], 71), 0),
        "tile_weight": scatter_about(streams_of[8], (BLOCKS, TPB, TILE, TILE), (TILE * TPB // 2) ** -0.5, 0.25, ((0, 64),)),
    }


def silu_slope(pre_value):
    sig = jax.nn.sigmoid(pre_value)
    return sig * (1.0 + pre_value * (1.0 - sig))

def live_slots(tile_index, tile_count):
    return lax.broadcasted_iota(jnp.int32, tile_index.shape, 1) < tile_count[:, None]

def device_forward(source, tile_index, tile_count, tile_weight):
    row_count = source.shape[0]
    width = tile_weight.shape[-1]
    blocked = source.reshape(row_count, source.shape[1] // width, width)
    picked = jnp.take(blocked, tile_index, axis=1)
    live = live_slots(tile_index, tile_count)
    picked = picked * live.astype(picked.dtype)[None, :, :, None]
    summed = jnp.einsum('fjsa,jsab->fjb', picked.astype(jnp.float32), tile_weight.astype(jnp.float32), precision=lax.Precision.HIGHEST)
    return summed.reshape(row_count, -1).astype(jnp.bfloat16)

def device_backward(grad_agg, tile_index, tile_count, tile_weight, src_count):
    row_count = grad_agg.shape[0]
    width = tile_weight.shape[-1]
    shaped = grad_agg.reshape(row_count, tile_index.shape[0], width)
    part_grad = jnp.einsum('fjb,jsab->fjsa', shaped.astype(jnp.float32), tile_weight.astype(jnp.float32), precision=lax.Precision.HIGHEST)
    live = live_slots(tile_index, tile_count)
    part_grad = part_grad * live.astype(jnp.float32)[None, :, :, None]
    empty = jnp.zeros((row_count, src_count, width), jnp.float32)
    filled = empty.at[:, tile_index.reshape(-1)].add(part_grad.reshape(row_count, -1, width))
    return filled.reshape(row_count, -1)

def reference(features, cotangent, w_self, w_neigh, send_index, send_count, tile_index, tile_count, tile_weight):
    grid = features.reshape(F, N_VERT, NLOC)
    hub_rows = grid[:, :, :HUB_DEV].reshape(F, HUBS)
    slot_live = lax.broadcasted_iota(jnp.int32, (N_VERT, N_VERT, SLOTS), 2) < send_count[:, :, None]
    owner_base = (lax.broadcasted_iota(jnp.int32, (N_VERT, N_VERT, SLOTS), 0) * NLOC).astype(jnp.int32)
    columns = (owner_base + send_index).astype(jnp.int32).reshape(-1)
    sent = jnp.take(features, columns, axis=1).reshape(F, N_VERT, N_VERT, SLOTS)
    sent = sent * slot_live.astype(features.dtype)[None]
    incoming = jnp.transpose(sent, (2, 0, 1, 3)).reshape(N_VERT, F, N_VERT * SLOTS)
    feat_dev = jnp.transpose(grid, (1, 0, 2))
    index_dev = tile_index.reshape(N_VERT, NT, TPB)
    count_dev = tile_count.reshape(N_VERT, NT)
    weight_dev = tile_weight.reshape(N_VERT, NT, TPB, TILE, TILE)

    def forward_one(pieces):
        own_feat, own_in, own_index, own_count, own_weight = pieces
        source = jnp.concatenate([own_feat, own_in, hub_rows], axis=1)
        return device_forward(source, own_index, own_count, own_weight)
    aggregate = lax.map(forward_one, (feat_dev, incoming, index_dev, count_dev, weight_dev))
    self_f = w_self.astype(jnp.float32)
    neigh_f = w_neigh.astype(jnp.float32)
    pre_value = jnp.einsum('fo,dfn->don', self_f, feat_dev.astype(jnp.float32), precision=lax.Precision.HIGHEST)
    pre_value = pre_value + jnp.einsum('fo,dfn->don', neigh_f, aggregate.astype(jnp.float32), precision=lax.Precision.HIGHEST)
    output_dev = jax.nn.silu(pre_value).astype(jnp.bfloat16)
    output = jnp.transpose(output_dev, (1, 0, 2)).reshape(FO, NODES)
    cot_dev = jnp.transpose(cotangent.reshape(FO, N_VERT, NLOC), (1, 0, 2))
    grad_pre = (cot_dev.astype(jnp.float32) * silu_slope(pre_value)).astype(jnp.bfloat16)
    grad_pre_f = grad_pre.astype(jnp.float32)
    scale = 1.0 / math.sqrt(NODES)
    grad_w_self = jnp.einsum('dfn,don->fo', feat_dev.astype(jnp.float32), grad_pre_f, precision=lax.Precision.HIGHEST) * scale
    grad_w_neigh = jnp.einsum('dfn,don->fo', aggregate.astype(jnp.float32), grad_pre_f, precision=lax.Precision.HIGHEST) * scale
    grad_direct = jnp.einsum('fo,don->dfn', self_f, grad_pre_f, precision=lax.Precision.HIGHEST)
    grad_agg = jnp.einsum('fo,don->dfn', neigh_f, grad_pre_f, precision=lax.Precision.HIGHEST).astype(jnp.bfloat16)
    edge = NLOC + N_VERT * SLOTS

    def backward_one(hub_total, pieces):
        own_grad, own_index, own_count, own_weight = pieces
        grad_source = device_backward(own_grad, own_index, own_count, own_weight, SRC_TILES)
        return (hub_total + grad_source[:, edge:], (grad_source[:, :NLOC], grad_source[:, NLOC:edge]))
    hub_total, (local_grad, recv_grad) = lax.scan(backward_one, jnp.zeros((F, HUBS), jnp.float32), (grad_agg, index_dev, count_dev, weight_dev))
    grad_x = jnp.transpose(grad_direct + local_grad, (1, 0, 2)).reshape(F, NODES)
    returned = jnp.transpose(recv_grad.reshape(N_VERT, F, N_VERT, SLOTS), (1, 2, 0, 3))
    returned = returned * slot_live.astype(jnp.float32)[None]
    grad_x = grad_x.at[:, columns].add(returned.reshape(F, -1))
    grad_x = grad_x.reshape(F, N_VERT, NLOC).at[:, :, :HUB_DEV].add(hub_total.reshape(F, N_VERT, HUB_DEV)).reshape(F, NODES)
    return (output, grad_x, grad_w_self, grad_w_neigh)
```

```python
import functools
import math

import jax
import jax.numpy as jnp
from jax import lax
from jax.experimental import pallas as pl
from jax.experimental.pallas import tpu as pltpu
from jax.sharding import PartitionSpec as P

T = 128
BF = jnp.bfloat16
F32 = jnp.float32
FIRST = (((0,), (0,)), ((), ()))
LAST = (((1,), (1,)), ((), ()))


def params(mib):
    return pltpu.CompilerParams(vmem_limit_bytes=mib * 2**20)


def low_lanes(rows):
    return lax.broadcasted_iota(jnp.int32, (rows, T), 1) < T // 2


def swap_halves(x):
    return pltpu.roll(x, T // 2, 1)


def onehot(index_row, base, nodes):
    row = lax.broadcasted_iota(jnp.int32, (nodes, index_row.shape[1]), 0)
    return jnp.where(row == index_row - base, F32(1), F32(0)).astype(BF)


def pick_kernel(feat_ref, index_ref, out_ref, *, chunk):
    rows, nodes = feat_ref.shape
    half = rows // 2
    hubs = feat_ref[:, :T]
    low = low_lanes(half)

    def body(t, carry):
        cols = pl.ds(pl.multiple_of(t * 2 * T, 2 * T), 2 * T)
        index_row = index_ref[:, cols]
        acc = jnp.zeros((rows, 2 * T), F32)
        for c in range(nodes // chunk):
            acc += jnp.dot(
                feat_ref[:, c * chunk : (c + 1) * chunk],
                onehot(index_row, c * chunk, chunk),
                preferred_element_type=F32,
            )
        for u in range(2):
            top = acc[:half, u * T : (u + 1) * T]
            bottom = acc[half:, u * T : (u + 1) * T]
            q = t * 4 + u * 2
            out_ref[q, :rows] = hubs
            out_ref[q + 1, :rows] = hubs
            out_ref[q, rows:] = jnp.where(low, top, swap_halves(bottom)).astype(BF)
            out_ref[q + 1, rows:] = jnp.where(low, swap_halves(top), bottom).astype(BF)
        return carry

    lax.fori_loop(0, index_ref.shape[1] // (2 * T), body, 0)


def forward_kernel(place_ref, feat_ref, recv_ref, weight_ref, out_ref, source):
    step = pl.program_id(0)
    rows, nodes = feat_ref.shape
    half = rows // 2
    peers = recv_ref.shape[0]
    own = nodes // T
    blocks = weight_ref.shape[0]
    slots = weight_ref.shape[1] // T

    @pl.when(step == 0)
    def _():
        low = low_lanes(half)
        for i in range(own):
            source[i] = feat_ref[:, i * T : (i + 1) * T]

        def pair(t, carry):
            a = recv_ref[2 * t, rows:].astype(F32)
            b = recv_ref[2 * t + 1, rows:].astype(F32)
            source[own + t, :half] = jnp.where(low, a, swap_halves(b)).astype(BF)
            source[own + t, half:] = jnp.where(low, swap_halves(a), b).astype(BF)
            source[own + peers // 2 + 2 * t] = recv_ref[2 * t, :rows]
            source[own + peers // 2 + 2 * t + 1] = recv_ref[2 * t + 1, :rows]
            return carry

        lax.fori_loop(0, peers // 2, pair, 0)
        source[own + peers // 2 + peers] = jnp.zeros((rows, T), BF)

    for j in range(blocks):
        at = (step * blocks + j) * slots
        picked = jnp.concatenate([source[place_ref[at + s]] for s in range(slots)], axis=1)
        total = jnp.dot(picked, weight_ref[j], preferred_element_type=F32)
        out_ref[0, :, j * T : (j + 1) * T] = total.astype(BF)


def dense_kernel(agg_ref, fc_ref, ws_ref, wn_ref, ga_ref, rest_ref, gw_ref):
    parts, rows, _ = agg_ref.shape
    agg = jnp.concatenate([agg_ref[r] for r in range(parts)], axis=0)
    feat = jnp.concatenate([fc_ref[r, :rows] for r in range(parts)], axis=0)
    ws = ws_ref[...]
    wn = wn_ref[...]
    pre = lax.dot_general(ws, feat, FIRST, preferred_element_type=F32)
    pre += lax.dot_general(wn, agg, FIRST, preferred_element_type=F32)
    cot = jnp.concatenate([fc_ref[r, rows:] for r in range(parts)], axis=0).astype(F32)
    sig = jax.nn.sigmoid(pre)
    out = (pre * sig).astype(BF)
    grad = (cot * (sig * (1.0 + pre * (1.0 - sig)))).astype(BF)
    grad_agg = jnp.dot(wn, grad, preferred_element_type=F32).astype(BF)
    direct = jnp.dot(ws, grad, preferred_element_type=F32).astype(BF)
    gself = lax.dot_general(feat, grad, LAST, preferred_element_type=F32)
    gneigh = lax.dot_general(agg, grad, LAST, preferred_element_type=F32)
    for r in range(parts):
        here = slice(r * rows, (r + 1) * rows)
        ga_ref[r] = grad_agg[here]
        rest_ref[r, :rows] = out[here]
        rest_ref[r, rows:] = direct[here]
        gw_ref[r, :, : gself.shape[1]] = gself[here]
        gw_ref[r, :, gself.shape[1] :] = gneigh[here]


def backward_kernel(place_ref, ga_ref, weight_ref, own_ref, send_ref, total, *, own, peers):
    step = pl.program_id(0)
    rows = ga_ref.shape[1]
    half = rows // 2
    blocks = weight_ref.shape[0]
    slots = weight_ref.shape[1] // T

    @pl.when(step == 0)
    def _():
        total[...] = jnp.zeros_like(total)

    for j in range(blocks):
        at = (step * blocks + j) * slots
        part = lax.dot_general(
            ga_ref[0, :, j * T : (j + 1) * T], weight_ref[j], LAST, preferred_element_type=F32
        )
        for s in range(slots):
            total[place_ref[at + s]] += part[:, s * T : (s + 1) * T]

    @pl.when(step == pl.num_programs(0) - 1)
    def _():
        low = low_lanes(half)
        for i in range(own):
            own_ref[:, i * T : (i + 1) * T] = total[i]

        def pair(t, carry):
            top = total[own + t, :half]
            bottom = total[own + t, half:]
            send_ref[2 * t, rows:] = jnp.where(low, top, swap_halves(bottom)).astype(BF)
            send_ref[2 * t + 1, rows:] = jnp.where(low, swap_halves(top), bottom).astype(BF)
            send_ref[2 * t, :rows] = total[own + peers // 2 + 2 * t].astype(BF)
            send_ref[2 * t + 1, :rows] = total[own + peers // 2 + 2 * t + 1].astype(BF)
            return carry

        lax.fori_loop(0, peers // 2, pair, 0)


def finish_kernel(recv_ref, index_ref, own_ref, direct_ref, grad_ref, out_ref, slots_ref, *, chunk):
    rows, nodes = own_ref.shape
    half = rows // 2
    peers = recv_ref.shape[0]
    parts = direct_ref.shape[0]
    span = nodes // parts
    low = low_lanes(half)
    for t in range(peers // 2):
        a = recv_ref[2 * t, rows:].astype(F32)
        b = recv_ref[2 * t + 1, rows:].astype(F32)
        slots_ref[:half, t * T : (t + 1) * T] = jnp.where(low, a, swap_halves(b)).astype(BF)
        slots_ref[half:, t * T : (t + 1) * T] = jnp.where(low, swap_halves(a), b).astype(BF)
    for r in range(parts):
        here = slice(r * span, (r + 1) * span)
        grad_ref[:, here] = own_ref[:, here] + direct_ref[r, rows:].astype(F32)
        out_ref[:, here] = direct_ref[r, :rows]
    hub = recv_ref[0, :rows].astype(F32)
    for p in range(1, peers):
        hub += recv_ref[p, :rows].astype(F32)
    grad_ref[:, :T] += hub
    slot_count = index_ref.shape[1]

    def body(t, carry):
        base = pl.multiple_of(t * 2 * T, 2 * T)
        acc = jnp.zeros((rows, 2 * T), F32)
        for c in range(slot_count // chunk):
            here = slice(c * chunk, (c + 1) * chunk)
            acc += lax.dot_general(
                slots_ref[:, here],
                onehot(index_ref[:, here], base, 2 * T),
                LAST,
                preferred_element_type=F32,
            )
        grad_ref[:, pl.ds(base, 2 * T)] += acc
        return carry

    lax.fori_loop(0, nodes // (2 * T), body, 0)


def whole(shape):
    return pl.BlockSpec(shape, lambda *_: (0,) * len(shape))


def local(
    features,
    cotangent,
    w_self,
    w_neigh,
    send_index,
    send_count,
    tile_index,
    tile_count,
    tile_weight,
):
    rows, nodes = features.shape
    peers = lax.axis_size("vert")
    parts = lax.axis_size("af")
    span = nodes // parts
    feat_out = w_self.shape[1]
    blocks, slots = tile_index.shape
    slot_count = send_index.shape[2]
    own = nodes // T
    sources = own + peers * slot_count // T + peers
    per_step = span // T
    half = rows // 2

    exchange = functools.partial(lax.all_to_all, split_axis=0, concat_axis=0, tiled=True)
    both = jnp.stack([features, cotangent]).reshape(2, rows, parts, span)
    both = jnp.transpose(both, (2, 0, 1, 3)).reshape(parts, 2 * rows, span)
    both = exchange(both, "af")

    slot_live = lax.broadcasted_iota(jnp.int32, (peers, slot_count), 1) < send_count.reshape(
        peers, 1
    )
    index_row = jnp.where(slot_live, send_index[0], -1).reshape(1, peers * slot_count)
    tile_live = lax.broadcasted_iota(jnp.int32, (blocks, slots), 1) < tile_count[:, None]
    place = jnp.where(tile_live, tile_index, sources).reshape(blocks * slots)
    weight = tile_weight.reshape(blocks, slots * T, T)

    send = pl.pallas_call(
        functools.partial(pick_kernel, chunk=512),
        out_shape=jax.ShapeDtypeStruct((peers, rows + half, T), BF),
        compiler_params=params(16),
        name="pick",
    )(features, index_row)
    recv = exchange(send, "vert")

    agg = pl.pallas_call(
        forward_kernel,
        grid_spec=pltpu.PrefetchScalarGridSpec(
            num_scalar_prefetch=1,
            grid=(parts,),
            in_specs=[
                whole((rows, nodes)),
                whole((peers, rows + half, T)),
                pl.BlockSpec((per_step, slots * T, T), lambda i, _: (i, 0, 0)),
            ],
            out_specs=pl.BlockSpec((1, rows, span), lambda i, _: (i, 0, 0)),
            scratch_shapes=[pltpu.VMEM((sources + 1, rows, T), BF)],
        ),
        out_shape=jax.ShapeDtypeStruct((parts, rows, span), BF),
        compiler_params=params(24),
        name="aggregate",
    )(place, features, recv, weight)
    agg = exchange(agg, "af")

    grad_agg, rest, gw = pl.pallas_call(
        dense_kernel,
        out_shape=(
            jax.ShapeDtypeStruct((parts, rows, span), BF),
            jax.ShapeDtypeStruct((parts, 2 * rows, span), BF),
            jax.ShapeDtypeStruct((parts, rows, 2 * feat_out), F32),
        ),
        compiler_params=params(32),
        name="dense",
    )(agg, both, w_self, w_neigh)
    grad_agg = exchange(grad_agg, "af")
    rest = exchange(rest, "af")

    gw = exchange(gw, "af").sum(axis=0)
    piece = rows * 2 * feat_out // (peers * T)
    gw = exchange(gw.reshape(peers, piece, T), "vert").sum(axis=0)
    gw = exchange(jnp.broadcast_to(gw[None], (peers, piece, T)), "vert")
    gw = gw.reshape(rows, 2 * feat_out) * (1.0 / math.sqrt(nodes * peers))

    own_grad, send = pl.pallas_call(
        functools.partial(backward_kernel, own=own, peers=peers),
        grid_spec=pltpu.PrefetchScalarGridSpec(
            num_scalar_prefetch=1,
            grid=(parts,),
            in_specs=[
                pl.BlockSpec((1, rows, span), lambda i, _: (i, 0, 0)),
                pl.BlockSpec((per_step, slots * T, T), lambda i, _: (i, 0, 0)),
            ],
            out_specs=[whole((rows, nodes)), whole((peers, rows + half, T))],
            scratch_shapes=[pltpu.VMEM((sources + 1, rows, T), F32)],
        ),
        out_shape=(
            jax.ShapeDtypeStruct((rows, nodes), F32),
            jax.ShapeDtypeStruct((peers, rows + half, T), BF),
        ),
        compiler_params=params(24),
        name="spread",
    )(place, grad_agg, weight)
    recv = exchange(send, "vert")

    grad_x, output = pl.pallas_call(
        functools.partial(finish_kernel, chunk=512),
        out_shape=(
            jax.ShapeDtypeStruct((rows, nodes), F32),
            jax.ShapeDtypeStruct((rows, nodes), BF),
        ),
        scratch_shapes=[pltpu.VMEM((rows, peers * slot_count), BF)],
        compiler_params=params(24),
        name="finish",
    )(recv, index_row, own_grad, rest)
    return output, grad_x, gw[:, :feat_out], gw[:, feat_out:]


def solution(mesh):
    in_specs = (
        P("af", "vert"),
        P("af", "vert"),
        P(),
        P(),
        P("vert", None, None),
        P("vert", None),
        P("vert", None),
        P("vert"),
        P("vert", None, None, None),
    )
    out_specs = (P("af", "vert"), P("af", "vert"), P("af", None), P("af", None))
    return jax.shard_map(local, mesh=mesh, in_specs=in_specs, out_specs=out_specs, check_vma=False)
```

```python
import functools
import math

import jax
import jax.numpy as jnp
from jax import lax
from jax.experimental import pallas as pl
from jax.experimental.pallas import tpu as pltpu
from jax.sharding import PartitionSpec as P

T = 128
BF = jnp.bfloat16
F32 = jnp.float32
FIRST = (((0,), (0,)), ((), ()))
LAST = (((1,), (1,)), ((), ()))


def params(mib):
    return pltpu.CompilerParams(vmem_limit_bytes=mib * 2**20)


def low_lanes(rows):
    return lax.broadcasted_iota(jnp.int32, (rows, T), 1) < T // 2


def swap_halves(x):
    return pltpu.roll(x, T // 2, 1)


def onehot(index_row, width):
    row = lax.broadcasted_iota(jnp.int16, (width, index_row.shape[1]), 0)
    low = jnp.where(index_row < 0, -1, index_row & (width - 1))
    return jnp.where(row == low.astype(jnp.int16), BF(1), BF(0))


def split_kernel(me_ref, array_ref, *outs):
    span = outs[0].shape[1]
    me = me_ref[0]
    for k, out_ref in enumerate(outs, 1):
        out_ref[...] = array_ref[:, pl.ds(pl.multiple_of((me ^ k) * span, span), span)]


def pick_kernel(feat_ref, index_ref, out_ref, stacked, *, width):
    rows, nodes = feat_ref.shape
    half = rows // 2
    low = low_lanes(half)
    for h in range(nodes // width):
        stacked[h * rows : (h + 1) * rows] = feat_ref[:, h * width : (h + 1) * width]

    def body(t, carry):
        cols = pl.ds(pl.multiple_of(t * 2 * T, 2 * T), 2 * T)
        index_row = index_ref[:, cols]
        high = jnp.broadcast_to(index_row >> (width.bit_length() - 1), (rows, 2 * T))
        found = jnp.dot(stacked[...], onehot(index_row, width), preferred_element_type=F32)
        found = [found[h * rows : (h + 1) * rows] for h in range(nodes // width)]
        while len(found) > 1:
            odd = (high & 1) != 0
            high = high >> 1
            found = [jnp.where(odd, b, a) for a, b in zip(found[::2], found[1::2])]
        acc = found[0]
        for u in range(2):
            top = acc[:half, u * T : (u + 1) * T]
            bottom = acc[half:, u * T : (u + 1) * T]
            q = t * 4 + u * 2
            out_ref[q] = jnp.where(low, top, swap_halves(bottom)).astype(BF)
            out_ref[q + 1] = jnp.where(low, swap_halves(top), bottom).astype(BF)
        return carry

    lax.fori_loop(0, index_ref.shape[1] // (2 * T), body, 0, unroll=2)


def forward_kernel(me_ref, place_ref, feat_ref, recv_ref, h0, h1, h2, h3, weight_ref, *refs):
    outs, (source, result) = refs[:4], refs[4:]
    step = pl.program_id(0)
    rows, nodes = feat_ref.shape
    half = rows // 2
    peers = recv_ref.shape[0]
    own = nodes // T
    blocks = weight_ref.shape[0]
    slots = weight_ref.shape[1] // T

    @pl.when(step == 0)
    def _():
        low = low_lanes(half)
        for i in range(own):
            source[i] = feat_ref[:, i * T : (i + 1) * T]

        def pair(t, carry):
            a = recv_ref[2 * t].astype(F32)
            b = recv_ref[2 * t + 1].astype(F32)
            source[own + t, :half] = jnp.where(low, a, swap_halves(b)).astype(BF)
            source[own + t, half:] = jnp.where(low, swap_halves(a), b).astype(BF)
            return carry

        lax.fori_loop(0, peers // 2, pair, 0)
        first = own + peers // 2
        for k, hub_ref in enumerate((h0, h1, h2, h3)):
            many = hub_ref.shape[0]
            source[first + k * many : first + (k + 1) * many] = hub_ref[...]
        source[first + peers] = jnp.zeros((rows, T), BF)

    first = (me_ref[0] ^ (3 - step)) * blocks
    for j in range(blocks):
        at = (first + j) * slots
        picked = jnp.concatenate([source[place_ref[at + s]] for s in range(slots)], axis=1)
        total = jnp.dot(picked, weight_ref[j], preferred_element_type=F32)
        result[:, j * T : (j + 1) * T] = total.astype(BF)
    for k in range(4):

        @pl.when(step == 3 - k)
        def _(k=k):
            outs[k][...] = result[...]


def dense_kernel(me_ref, *refs):
    aggs, feat_ref, cot_ref, feats, cots = refs[:4], refs[4], refs[5], refs[6:9], refs[9:12]
    ws_ref, wn_ref, gas, rests = refs[12], refs[13], refs[14:18], refs[18:22]
    agg_s, feat_s, cot_s, out_s, dir_s, gw_s = refs[22:]
    rows = feat_ref.shape[0]
    me = me_ref[0]
    at = [pl.ds(pl.multiple_of((me ^ k) * rows, rows), rows) for k in range(4)]
    feat_s[at[0]] = feat_ref[...]
    cot_s[at[0]] = cot_ref[...]
    for k in range(4):
        agg_s[at[k]] = aggs[k][...]
        if k:
            feat_s[at[k]] = feats[k - 1][...]
            cot_s[at[k]] = cots[k - 1][...]
    agg = agg_s[...]
    feat = feat_s[...]
    ws = ws_ref[...]
    wn = wn_ref[...]
    pre = lax.dot_general(ws, feat, FIRST, preferred_element_type=F32)
    pre += lax.dot_general(wn, agg, FIRST, preferred_element_type=F32)
    sig = jax.nn.sigmoid(pre)
    out_s[...] = (pre * sig).astype(BF)
    grad = (cot_s[...].astype(F32) * (sig * (1.0 + pre * (1.0 - sig)))).astype(BF)
    agg_s[...] = jnp.dot(wn, grad, preferred_element_type=F32).astype(BF)
    dir_s[...] = jnp.dot(ws, grad, preferred_element_type=F32).astype(BF)
    wide = ws.shape[1]
    gw_s[:, :wide] = lax.dot_general(feat, grad, LAST, preferred_element_type=F32).astype(BF)
    gw_s[:, wide:] = lax.dot_general(agg, grad, LAST, preferred_element_type=F32).astype(BF)
    for k in range(4):
        gas[k][:rows] = agg_s[at[k]]
        mine = gw_s[at[k]]
        gas[k][rows:, : 2 * wide] = mine[: rows // 2]
        gas[k][rows:, 2 * wide :] = mine[rows // 2 :]
        rests[k][:rows] = out_s[at[k]]
        rests[k][rows:] = dir_s[at[k]]


def backward_kernel(me_ref, place_ref, g0, g1, g2, g3, weight_ref, *refs, own, peers):
    own_ref, send_ref, hub0, hub1, hub2, hub3, total, grads = refs
    step = pl.program_id(0)
    rows = own_ref.shape[0]
    half = rows // 2
    blocks = weight_ref.shape[0]
    slots = weight_ref.shape[1] // T

    @pl.when(step == 0)
    def _():
        total[...] = jnp.zeros_like(total)
        for k, grad_ref in enumerate((g0, g1, g2, g3)):
            grads[k] = grad_ref[:rows]

    first = (me_ref[0] ^ step) * blocks
    for j in range(blocks):
        at = (first + j) * slots
        part = lax.dot_general(
            grads[step, :, j * T : (j + 1) * T], weight_ref[j], LAST, preferred_element_type=F32
        )
        for s in range(slots):
            total[place_ref[at + s]] += part[:, s * T : (s + 1) * T]

    @pl.when(step == pl.num_programs(0) - 1)
    def _():
        low = low_lanes(half)
        for i in range(own):
            own_ref[:, i * T : (i + 1) * T] = total[i]

        def pair(t, carry):
            top = total[own + t, :half]
            bottom = total[own + t, half:]
            send_ref[2 * t] = jnp.where(low, top, swap_halves(bottom)).astype(BF)
            send_ref[2 * t + 1] = jnp.where(low, swap_halves(top), bottom).astype(BF)
            return carry

        lax.fori_loop(0, peers // 2, pair, 0)
        many = peers // 4
        for k, hub_ref in enumerate((hub0, hub1, hub2, hub3)):
            start = own + peers // 2 + k * many
            hub_ref[:many] = total[start : start + many].astype(hub_ref.dtype)
        wide = g0.shape[1] // 2
        for u in range(2):
            here = slice(u * wide, (u + 1) * wide)
            g = [x[rows:, here].astype(F32) for x in (g0, g1, g2, g3)]
            gw = ((g[0] + g[1]) + (g[2] + g[3])).astype(BF)
            for c in range(wide // T):
                part = gw[:, c * T : (c + 1) * T]
                for hub_ref in (hub0, hub1, hub2, hub3):
                    hub_ref[many + c, u * half : (u + 1) * half] = part.astype(hub_ref.dtype)


def finish_kernel(me_ref, recv_ref, index_ref, own_ref, *refs, width, chunk, scale):
    rests, hubs = refs[:4], refs[4:8]
    grad_ref, out_ref, gself_ref, gneigh_ref, slots_ref, acc_ref = refs[8:]
    rows, nodes = own_ref.shape
    half = rows // 2
    peers = recv_ref.shape[0]
    span = rests[0].shape[1]
    low = low_lanes(half)
    me = me_ref[0]
    for t in range(peers // 2):
        a = recv_ref[2 * t].astype(F32)
        b = recv_ref[2 * t + 1].astype(F32)
        slots_ref[:half, t * T : (t + 1) * T] = jnp.where(low, a, swap_halves(b)).astype(BF)
        slots_ref[half:, t * T : (t + 1) * T] = jnp.where(low, swap_halves(a), b).astype(BF)
    for k in range(4):
        here = pl.ds(pl.multiple_of((me ^ k) * span, span), span)
        grad_ref[:, here] = own_ref[:, here] + rests[k][rows:].astype(F32)
        out_ref[:, here] = rests[k][:rows]
    many = nodes // width
    acc_ref[...] = jnp.zeros_like(acc_ref)

    def body(t, carry):
        cols = pl.ds(pl.multiple_of(t * chunk, chunk), chunk)
        index_row = index_ref[:, cols]
        high = jnp.broadcast_to(index_row >> (width.bit_length() - 1), (rows, chunk)).astype(jnp.int16)
        values = slots_ref[:, cols]
        spread = jnp.concatenate([jnp.where(high == h, values, BF(0)) for h in range(many)], axis=0)
        acc_ref[...] += lax.dot_general(
            spread, onehot(index_row, width), LAST, preferred_element_type=F32
        )
        return carry

    lax.fori_loop(0, index_ref.shape[1] // chunk, body, 0)
    for h in range(many):
        grad_ref[:, h * width : (h + 1) * width] += acc_ref[h * rows : (h + 1) * rows]
    total = [
        (hubs[0][c] + hubs[1][c].astype(F32)) + (hubs[2][c].astype(F32) + hubs[3][c].astype(F32))
        for c in range(hubs[0].shape[0])
    ]
    grad_ref[:, :T] += total[0]
    wide = gself_ref.shape[1] // T
    for c in range(wide):
        gself_ref[:, c * T : (c + 1) * T] = total[1 + c] * scale
        gneigh_ref[:, c * T : (c + 1) * T] = total[1 + wide + c] * scale

def add_kernel(own_ref, one_ref, two_ref, three_ref, *outs):
    wide = outs[0].shape[0] * len(outs) - own_ref.shape[0]
    wide = wide // (len(outs) - 1)
    many = own_ref.shape[0] - wide
    for i in range(many + wide):
        total = (own_ref[i] + one_ref[i].astype(F32)) + (two_ref[i].astype(F32) + three_ref[i].astype(F32))
        if i < many:
            out_ref = outs[i * len(outs) // many]
            out_ref[i % (many // len(outs))] = total.astype(out_ref.dtype)
        else:
            total = total.astype(BF)
            for out_ref in outs:
                out_ref[many // len(outs) + i - many] = total.astype(out_ref.dtype)


def whole(shape):
    return pl.BlockSpec(shape, lambda *_: (0,) * len(shape))


def shape_of(*shape, dtype=BF):
    return jax.ShapeDtypeStruct(shape, dtype)


def call(kernel, name, prefetch, out_shape, operands, in_specs=None, grid=(1,), scratch=(), mib=24, micros=0):
    in_specs = in_specs or {}
    return pl.pallas_call(
        kernel,
        grid_spec=pltpu.PrefetchScalarGridSpec(
            num_scalar_prefetch=len(prefetch),
            grid=grid,
            in_specs=[in_specs.get(i) or whole(x.shape) for i, x in enumerate(operands)],
            out_specs=[whole(s.shape) for s in out_shape],
            scratch_shapes=[pltpu.VMEM(s.shape, s.dtype) for s in scratch],
        ),
        out_shape=tuple(out_shape),
        compiler_params=params(mib),
        cost_estimate=pl.CostEstimate(
            flops=int(micros * 1e9), bytes_accessed=int(micros * 3e6), transcendentals=0
        ) if micros else None,
        name=name,
    )(*prefetch, *operands)


def local(
    features,
    cotangent,
    w_self,
    w_neigh,
    send_index,
    send_count,
    tile_index,
    tile_count,
    tile_weight,
):
    rows, nodes = features.shape
    peers = lax.axis_size("vert")
    parts = lax.axis_size("af")
    span = nodes // parts
    feat_out = w_self.shape[1]
    blocks, slots = tile_index.shape
    slot_count = send_index.shape[2]
    own = nodes // T
    first_hub = own + peers * slot_count // T
    sources = first_hub + peers
    per_step = span // T
    half = rows // 2
    vert = lax.axis_index("vert")
    me = lax.axis_index("af").astype(jnp.int32).reshape(1)

    def swap(x, axis, mask):
        size = peers if axis == "vert" else parts
        return lax.ppermute(x, axis, [(i, i ^ mask) for i in range(size)])

    def swap3(x, axis, unit):
        return [swap(x, axis, k * unit) for k in (1, 2, 3)]

    plane = peers // 4
    groups = [[y * plane + i for i in range(plane)] for y in range(4)]
    hub = jnp.broadcast_to(features[None, :, :T], (plane, rows, T))
    hub = lax.all_to_all(hub, "vert", 0, 0, axis_index_groups=groups, tiled=True)

    def split(x):
        parts_out = call(split_kernel, "split", (me,), [shape_of(rows, span)] * 3, (x,))
        return [swap(part, "af", k) for k, part in enumerate(parts_out, 1)]

    feats = split(features)
    cots = split(cotangent)

    slot_live = lax.broadcasted_iota(jnp.int32, (peers, slot_count), 1) < send_count.reshape(
        peers, 1
    )
    index_row = jnp.where(slot_live, send_index[0], -1).reshape(1, peers * slot_count)
    tile_live = lax.broadcasted_iota(jnp.int32, (blocks, slots), 1) < tile_count[:, None]
    def turned(mask):
        turn = ((tile_index - first_hub) ^ mask) + first_hub
        turn = jnp.where(tile_index >= first_hub, turn, tile_index)
        return jnp.where(tile_live, turn, sources).reshape(blocks * slots)

    place = turned(vert & (3 * plane))
    place_back = turned(vert)
    weight = tile_weight.reshape(blocks, slots * T, T)

    (send,) = call(
        functools.partial(pick_kernel, width=2 * T),
        "pick",
        (),
        [shape_of(peers, half, T)],
        (features, index_row),
        micros=30,
        scratch=[shape_of(rows * nodes // (2 * T), 2 * T)],
    )
    send, hub, feats = lax.optimization_barrier((send, hub, feats))
    hubs = [hub] + swap3(hub, "vert", 16)
    recv = lax.all_to_all(send, "vert", 0, 0, tiled=True)
    recv, cots = lax.optimization_barrier((recv, cots))

    agg = call(
        forward_kernel,
        "aggregate",
        (me, place),
        [shape_of(rows, span)] * 4,
        (features, recv, *hubs, weight),
        {6: pl.BlockSpec((per_step, slots * T, T), lambda i, me, _: (me[0] ^ (3 - i), 0, 0))},
        (parts,),
        [shape_of(sources + 1, rows, T), shape_of(rows, span)],
        mib=48,
    )
    agg = [x if k == 0 else swap(x, "af", k) for k, x in enumerate(agg)]

    mine = pl.BlockSpec((rows, span), lambda i, me: (0, me[0]))
    full = shape_of(parts * rows, span)
    dense = call(
        dense_kernel,
        "dense",
        (me,),
        [shape_of(rows + half, span)] * 4 + [shape_of(2 * rows, span)] * 4,
        (*agg, features, cotangent, *feats, *cots, w_self, w_neigh),
        {4: mine, 5: mine},
        scratch=[full] * 5 + [shape_of(parts * rows, 2 * feat_out)],
        mib=32,
    )
    grad_agg, rest = (
        [x if k == 0 else swap(x, "af", k) for k, x in enumerate(dense[i : i + 4])] for i in (0, 4)
    )
    grad_agg, rest[1:3] = lax.optimization_barrier((grad_agg, rest[1:3]))
    many = peers // 4
    wide = 2 * feat_out // T
    own_grad, send, *sent = call(
        functools.partial(backward_kernel, own=own, peers=peers),
        "spread",
        (me, place_back),
        [shape_of(rows, nodes, dtype=F32), shape_of(peers, half, T)]
        + [shape_of(many + wide, rows, T, dtype=F32)]
        + [shape_of(many + wide, rows, T)] * 3,
        (*grad_agg, weight),
        {4: pl.BlockSpec((per_step, slots * T, T), lambda i, me, _: (me[0] ^ i, 0, 0))},
        (parts,),
        [shape_of(sources + 1, rows, T, dtype=F32), shape_of(parts, rows, span)],
        mib=48,
        micros=30,
    )
    recv = lax.all_to_all(send, "vert", 0, 0, tiled=True)
    sent = [x if k == 0 else swap(x, "vert", 16 * k) for k, x in enumerate(sent)]
    for unit in (4, 1):
        sent = call(
            add_kernel,
            "add",
            (),
            [shape_of(unit + wide, rows, T, dtype=F32)] + [shape_of(unit + wide, rows, T)] * 3,
            sent,
            micros=30 if unit > 1 else 0,
        )
        sent = [x if k == 0 else swap(x, "vert", unit * k) for k, x in enumerate(sent)]

    grad_x, output, gself, gneigh = call(
        functools.partial(
            finish_kernel, width=2 * T, chunk=512, scale=1.0 / math.sqrt(nodes * peers)
        ),
        "finish",
        (me,),
        [
            shape_of(rows, nodes, dtype=F32),
            shape_of(rows, nodes),
            shape_of(rows, feat_out, dtype=F32),
            shape_of(rows, feat_out, dtype=F32),
        ],
        (recv, index_row, own_grad, *rest, *sent),
        scratch=[
            shape_of(rows, peers * slot_count),
            shape_of(rows * nodes // (2 * T), 2 * T, dtype=F32),
        ],
    )
    return output, grad_x, gself, gneigh


def solution(mesh):
    in_specs = (
        P("af", "vert"),
        P("af", "vert"),
        P(),
        P(),
        P("vert", None, None),
        P("vert", None),
        P("vert", None),
        P("vert"),
        P("vert", None, None, None),
    )
    out_specs = (P("af", "vert"), P("af", "vert"), P("af", None), P("af", None))
    return jax.shard_map(local, mesh=mesh, in_specs=in_specs, out_specs=out_specs, check_vma=False)
```

```python
import functools
import math

import jax
import jax.numpy as jnp
from jax import lax
from jax.experimental import pallas as pl
from jax.experimental.pallas import tpu as pltpu
from jax.sharding import PartitionSpec as P

T = 128
BF = jnp.bfloat16
F32 = jnp.float32
FIRST = (((0,), (0,)), ((), ()))
LAST = (((1,), (1,)), ((), ()))


def params(mib):
    return pltpu.CompilerParams(vmem_limit_bytes=mib * 2**20)


def low_lanes(rows):
    return lax.broadcasted_iota(jnp.int32, (rows, T), 1) < T // 2


def swap_halves(x):
    return pltpu.roll(x, T // 2, 1)


def onehot(index_row, width):
    row = lax.broadcasted_iota(jnp.int16, (width, index_row.shape[1]), 0)
    low = jnp.where(index_row < 0, -1, index_row & (width - 1))
    return jnp.where(row == low.astype(jnp.int16), BF(1), BF(0))


def pick_kernel(feat_ref, index_ref, out_ref, stacked, *, width):
    rows, nodes = feat_ref.shape
    half = rows // 2
    low = low_lanes(half)
    for h in range(nodes // width):
        stacked[h * rows : (h + 1) * rows] = feat_ref[:, h * width : (h + 1) * width]

    def body(t, carry):
        cols = pl.ds(pl.multiple_of(t * 2 * T, 2 * T), 2 * T)
        index_row = index_ref[:, cols]
        high = jnp.broadcast_to(index_row >> (width.bit_length() - 1), (rows, 2 * T))
        found = jnp.dot(stacked[...], onehot(index_row, width), preferred_element_type=F32)
        found = [found[h * rows : (h + 1) * rows] for h in range(nodes // width)]
        while len(found) > 1:
            odd = (high & 1) != 0
            high = high >> 1
            found = [jnp.where(odd, b, a) for a, b in zip(found[::2], found[1::2])]
        acc = found[0]
        for u in range(2):
            top = acc[:half, u * T : (u + 1) * T]
            bottom = acc[half:, u * T : (u + 1) * T]
            q = t * 4 + u * 2
            out_ref[q] = jnp.where(low, top, swap_halves(bottom)).astype(BF)
            out_ref[q + 1] = jnp.where(low, swap_halves(top), bottom).astype(BF)
        return carry

    lax.fori_loop(0, index_ref.shape[1] // (2 * T), body, 0, unroll=2)


def forward_kernel(place_ref, feat_ref, recv_ref, h0, h1, h2, h3, weight_ref, out_ref, source):
    step = pl.program_id(0)
    rows, nodes = feat_ref.shape
    half = rows // 2
    peers = recv_ref.shape[0]
    own = nodes // T
    blocks = weight_ref.shape[0]
    slots = weight_ref.shape[1] // T

    @pl.when(step == 0)
    def _():
        low = low_lanes(half)
        for i in range(own):
            source[i] = feat_ref[:, i * T : (i + 1) * T]

        def pair(t, carry):
            a = recv_ref[2 * t].astype(F32)
            b = recv_ref[2 * t + 1].astype(F32)
            source[own + t, :half] = jnp.where(low, a, swap_halves(b)).astype(BF)
            source[own + t, half:] = jnp.where(low, swap_halves(a), b).astype(BF)
            return carry

        lax.fori_loop(0, peers // 2, pair, 0)
        first = own + peers // 2
        for k, hub_ref in enumerate((h0, h1, h2, h3)):
            many = hub_ref.shape[0]
            source[first + k * many : first + (k + 1) * many] = hub_ref[...]
        source[first + peers] = jnp.zeros((rows, T), BF)

    for j in range(blocks):
        at = (step * blocks + j) * slots
        picked = jnp.concatenate([source[place_ref[at + s]] for s in range(slots)], axis=1)
        total = jnp.dot(picked, weight_ref[j], preferred_element_type=F32)
        out_ref[:, j * T : (j + 1) * T] = total.astype(BF)


def partial_kernel(me_ref, feat_ref, feat2_ref, agg_ref, agg2_ref, ws_ref, wn_ref, own_ref, s0, s1, stack):
    rows, nodes = feat_ref.shape
    me = me_ref[0]
    mine = pl.multiple_of((me & 1) * rows, rows)
    other = pl.multiple_of(rows - (me & 1) * rows, rows)
    chip = pl.ds(pl.multiple_of((me >> 1) * 2 * rows, 2 * rows), 2 * rows)
    for base, one, two in ((0, feat_ref, feat2_ref), (2 * rows, agg_ref, agg2_ref)):
        stack[pl.ds(base + mine, rows)] = one[...]
        stack[pl.ds(base + other, rows)] = two[...]
    outs = [pl.ds(pl.multiple_of((me ^ k) * rows, rows), rows) for k in (0, 2)]
    left = jnp.concatenate(
        [jnp.concatenate([ws_ref[o, chip], wn_ref[o, chip]], axis=1) for o in outs], axis=0
    )
    span = nodes // 4
    for i in range(4):
        here = slice(i * span, (i + 1) * span)
        part = jnp.dot(left, stack[:, here], preferred_element_type=F32)
        own_ref[:, here] = part[:rows]
        (s0, s1)[i // 2][:, (i % 2) * span : (i % 2 + 1) * span] = part[rows:].astype(BF)


def act_kernel(own_ref, recv_ref, cot_ref, out_ref, grad_ref):
    pre = own_ref[...] + recv_ref[...].astype(F32)
    sig = jax.nn.sigmoid(pre)
    out_ref[...] = (pre * sig).astype(BF)
    grad_ref[...] = (cot_ref[...].astype(F32) * (sig * (1.0 + pre * (1.0 - sig)))).astype(BF)


def back_kernel(me_ref, *refs):
    grads, (feat_ref, agg_ref, ws_ref, wn_ref, ga_ref, dir_ref, gw_ref, stack) = refs[:8], refs[8:]
    rows, nodes = feat_ref.shape
    me = me_ref[0]
    half = nodes // 2
    for k in range(4):
        at = pl.ds(pl.multiple_of((me ^ k) * rows, rows), rows)
        for h in range(2):
            stack[at, h * half : (h + 1) * half] = grads[2 * k + h][...]
    mine = pl.ds(pl.multiple_of(me * rows, rows), rows)
    span = nodes // 4
    gself = gneigh = 0.0
    for i in range(4):
        here = slice(i * span, (i + 1) * span)
        grad = stack[:, here]
        ga_ref[:, here] = jnp.dot(wn_ref[mine], grad, preferred_element_type=F32).astype(BF)
        dir_ref[:, here] = jnp.dot(ws_ref[mine], grad, preferred_element_type=F32)
        gself += lax.dot_general(feat_ref[:, here], grad, LAST, preferred_element_type=F32)
        gneigh += lax.dot_general(agg_ref[:, here], grad, LAST, preferred_element_type=F32)
    wide = gself.shape[1]
    gw_ref[:, :wide] = gself
    gw_ref[:, wide:] = gneigh


def backward_kernel(place_ref, ga_ref, dir_ref, gw_ref, weight_ref, *refs, own, peers):
    own_ref, send_ref, hub0, hub1, hub2, hub3, total = refs
    step = pl.program_id(0)
    rows = own_ref.shape[0]
    half = rows // 2
    blocks = weight_ref.shape[0]
    slots = weight_ref.shape[1] // T

    @pl.when(step == 0)
    def _():
        total[...] = jnp.zeros_like(total)

    for j in range(blocks):
        at = (step * blocks + j) * slots
        part = lax.dot_general(
            ga_ref[:, j * T : (j + 1) * T], weight_ref[j], LAST, preferred_element_type=F32
        )
        for s in range(slots):
            total[place_ref[at + s]] += part[:, s * T : (s + 1) * T]

    @pl.when(step == pl.num_programs(0) - 1)
    def _():
        low = low_lanes(half)
        for i in range(own):
            own_ref[:, i * T : (i + 1) * T] = total[i] + dir_ref[:, i * T : (i + 1) * T]

        def pair(t, carry):
            top = total[own + t, :half]
            bottom = total[own + t, half:]
            send_ref[2 * t] = jnp.where(low, top, swap_halves(bottom)).astype(BF)
            send_ref[2 * t + 1] = jnp.where(low, swap_halves(top), bottom).astype(BF)
            return carry

        lax.fori_loop(0, peers // 2, pair, 0)
        many = peers // 4
        for k, hub_ref in enumerate((hub0, hub1, hub2, hub3)):
            start = own + peers // 2 + k * many
            hub_ref[:many] = total[start : start + many].astype(hub_ref.dtype)
        for c in range(gw_ref.shape[1] // T):
            part = gw_ref[:, c * T : (c + 1) * T].astype(BF)
            for hub_ref in (hub0, hub1, hub2, hub3):
                hub_ref[many + c] = part.astype(hub_ref.dtype)


def finish_kernel(recv_ref, index_ref, own_ref, out0, out1, *refs, width, chunk, scale):
    hubs = refs[:4]
    grad_ref, out_ref, gself_ref, gneigh_ref, slots_ref, acc_ref = refs[4:]
    rows, nodes = own_ref.shape
    half = rows // 2
    peers = recv_ref.shape[0]
    low = low_lanes(half)
    for t in range(peers // 2):
        a = recv_ref[2 * t].astype(F32)
        b = recv_ref[2 * t + 1].astype(F32)
        slots_ref[:half, t * T : (t + 1) * T] = jnp.where(low, a, swap_halves(b)).astype(BF)
        slots_ref[half:, t * T : (t + 1) * T] = jnp.where(low, swap_halves(a), b).astype(BF)
    out_ref[:, : nodes // 2] = out0[...]
    out_ref[:, nodes // 2 :] = out1[...]
    grad_ref[...] = own_ref[...]
    many = nodes // width
    acc_ref[...] = jnp.zeros_like(acc_ref)

    def body(t, carry):
        cols = pl.ds(pl.multiple_of(t * chunk, chunk), chunk)
        index_row = index_ref[:, cols]
        high = jnp.broadcast_to(index_row >> (width.bit_length() - 1), (rows, chunk)).astype(jnp.int16)
        values = slots_ref[:, cols]
        spread = jnp.concatenate([jnp.where(high == h, values, BF(0)) for h in range(many)], axis=0)
        acc_ref[...] += lax.dot_general(
            spread, onehot(index_row, width), LAST, preferred_element_type=F32
        )
        return carry

    lax.fori_loop(0, index_ref.shape[1] // chunk, body, 0)
    for h in range(many):
        grad_ref[:, h * width : (h + 1) * width] += acc_ref[h * rows : (h + 1) * rows]
    total = [
        (hubs[0][c] + hubs[1][c].astype(F32)) + (hubs[2][c].astype(F32) + hubs[3][c].astype(F32))
        for c in range(hubs[0].shape[0])
    ]
    grad_ref[:, :T] += total[0]
    wide = gself_ref.shape[1] // T
    for c in range(wide):
        gself_ref[:, c * T : (c + 1) * T] = total[1 + c] * scale
        gneigh_ref[:, c * T : (c + 1) * T] = total[1 + wide + c] * scale

def add_kernel(own_ref, one_ref, two_ref, three_ref, *outs):
    wide = outs[0].shape[0] * len(outs) - own_ref.shape[0]
    wide = wide // (len(outs) - 1)
    many = own_ref.shape[0] - wide
    for i in range(many + wide):
        total = (own_ref[i] + one_ref[i].astype(F32)) + (two_ref[i].astype(F32) + three_ref[i].astype(F32))
        if i < many:
            out_ref = outs[i * len(outs) // many]
            out_ref[i % (many // len(outs))] = total.astype(out_ref.dtype)
        else:
            total = total.astype(BF)
            for out_ref in outs:
                out_ref[many // len(outs) + i - many] = total.astype(out_ref.dtype)


def whole(shape):
    return pl.BlockSpec(shape, lambda *_: (0,) * len(shape))


def shape_of(*shape, dtype=BF):
    return jax.ShapeDtypeStruct(shape, dtype)


def call(kernel, name, prefetch, out_shape, operands, in_specs=None, grid=(1,), scratch=(), mib=24, micros=0, out_specs=None):
    in_specs = in_specs or {}
    return pl.pallas_call(
        kernel,
        grid_spec=pltpu.PrefetchScalarGridSpec(
            num_scalar_prefetch=len(prefetch),
            grid=grid,
            in_specs=[in_specs.get(i) or whole(x.shape) for i, x in enumerate(operands)],
            out_specs=out_specs or [whole(s.shape) for s in out_shape],
            scratch_shapes=[pltpu.VMEM(s.shape, s.dtype) for s in scratch],
        ),
        out_shape=tuple(out_shape),
        compiler_params=params(mib),
        cost_estimate=pl.CostEstimate(
            flops=int(micros * 1e9), bytes_accessed=int(micros * 3e6), transcendentals=0
        ) if micros else None,
        name=name,
    )(*prefetch, *operands)


def local(
    features,
    cotangent,
    w_self,
    w_neigh,
    send_index,
    send_count,
    tile_index,
    tile_count,
    tile_weight,
):
    rows, nodes = features.shape
    peers = lax.axis_size("vert")
    parts = lax.axis_size("af")
    span = nodes // parts
    feat_out = w_self.shape[1]
    blocks, slots = tile_index.shape
    slot_count = send_index.shape[2]
    own = nodes // T
    first_hub = own + peers * slot_count // T
    sources = first_hub + peers
    per_step = span // T
    half = rows // 2
    vert = lax.axis_index("vert")
    me = lax.axis_index("af").astype(jnp.int32).reshape(1)

    def swap(x, axis, mask):
        size = peers if axis == "vert" else parts
        return lax.ppermute(x, axis, [(i, i ^ mask) for i in range(size)])

    def swap3(x, axis, unit):
        return [swap(x, axis, k * unit) for k in (1, 2, 3)]

    plane = peers // 4
    groups = [[y * plane + i for i in range(plane)] for y in range(4)]
    hub = jnp.broadcast_to(features[None, :, :T], (plane, rows, T))
    hub = lax.all_to_all(hub, "vert", 0, 0, axis_index_groups=groups, tiled=True)

    features2 = swap(features, "af", 1)

    slot_live = lax.broadcasted_iota(jnp.int32, (peers, slot_count), 1) < send_count.reshape(
        peers, 1
    )
    index_row = jnp.where(slot_live, send_index[0], -1).reshape(1, peers * slot_count)
    tile_live = lax.broadcasted_iota(jnp.int32, (blocks, slots), 1) < tile_count[:, None]
    def turned(mask):
        turn = ((tile_index - first_hub) ^ mask) + first_hub
        turn = jnp.where(tile_index >= first_hub, turn, tile_index)
        return jnp.where(tile_live, turn, sources).reshape(blocks * slots)

    place = turned(vert & (3 * plane))
    place_back = turned(vert)
    weight = tile_weight.reshape(blocks, slots * T, T)

    (send,) = call(
        functools.partial(pick_kernel, width=2 * T),
        "pick",
        (),
        [shape_of(peers, half, T)],
        (features, index_row),
        micros=30,
        scratch=[shape_of(rows * nodes // (2 * T), 2 * T)],
    )
    send, hub, features2 = lax.optimization_barrier((send, hub, features2))
    hubs = [hub] + swap3(hub, "vert", 16)
    recv = lax.all_to_all(send, "vert", 0, 0, tiled=True)

    blocked = pl.BlockSpec((per_step, slots * T, T), lambda i, place: (i, 0, 0))
    (agg,) = call(
        forward_kernel,
        "aggregate",
        (place,),
        [shape_of(rows, nodes)],
        (features, recv, *hubs, weight),
        {6: blocked},
        (parts,),
        [shape_of(sources + 1, rows, T)],
        mib=48,
        out_specs=[pl.BlockSpec((rows, span), lambda i, place: (0, i))],
    )
    agg2 = swap(agg, "af", 1)

    pre, *shares = call(
        partial_kernel,
        "partial",
        (me,),
        [shape_of(rows, nodes, dtype=F32)] + [shape_of(rows, nodes // 2)] * 2,
        (features, features2, agg, agg2, w_self.T, w_neigh.T),
        scratch=[shape_of(parts * rows, nodes)],
    )
    shares = [swap(x, "af", 2) for x in shares]
    outs, grads = [], []
    for h in range(2):
        column = pl.BlockSpec((rows, nodes // 2), functools.partial(lambda h, i: (0, h), h))
        out, grad = call(
            act_kernel,
            "act",
            (),
            [shape_of(rows, nodes // 2)] * 2,
            (pre, shares[h], cotangent),
            {0: column, 2: column},
        )
        outs.append(out)
        grads.append(grad)
    far = [swap(x, "af", 2) for x in grads]
    near = [swap(x, "af", 1) for x in grads]
    diagonal = [swap(x, "af", 1) for x in far]

    grad_agg, direct, gw = call(
        back_kernel,
        "back",
        (me,),
        [
            shape_of(rows, nodes),
            shape_of(rows, nodes, dtype=F32),
            shape_of(rows, 2 * feat_out, dtype=F32),
        ],
        (*grads, *near, *far, *diagonal, features, agg, w_self, w_neigh),
        scratch=[shape_of(parts * rows, nodes)],
    )

    many = peers // 4
    wide = 2 * feat_out // T
    own_grad, send, *sent = call(
        functools.partial(backward_kernel, own=own, peers=peers),
        "spread",
        (place_back,),
        [shape_of(rows, nodes, dtype=F32), shape_of(peers, half, T)]
        + [shape_of(many + wide, rows, T, dtype=F32)]
        + [shape_of(many + wide, rows, T)] * 3,
        (grad_agg, direct, gw, weight),
        {0: pl.BlockSpec((rows, span), lambda i, place: (0, i)), 3: blocked},
        (parts,),
        [shape_of(sources + 1, rows, T, dtype=F32)],
        mib=48,
        micros=30,
    )
    recv = lax.all_to_all(send, "vert", 0, 0, tiled=True)
    sent = [x if k == 0 else swap(x, "vert", 16 * k) for k, x in enumerate(sent)]
    for unit in (4, 1):
        sent = call(
            add_kernel,
            "add",
            (),
            [shape_of(unit + wide, rows, T, dtype=F32)] + [shape_of(unit + wide, rows, T)] * 3,
            sent,
            micros=30 if unit > 1 else 0,
        )
        sent = [x if k == 0 else swap(x, "vert", unit * k) for k, x in enumerate(sent)]

    grad_x, output, gself, gneigh = call(
        functools.partial(
            finish_kernel, width=2 * T, chunk=512, scale=1.0 / math.sqrt(nodes * peers)
        ),
        "finish",
        (),
        [
            shape_of(rows, nodes, dtype=F32),
            shape_of(rows, nodes),
            shape_of(rows, feat_out, dtype=F32),
            shape_of(rows, feat_out, dtype=F32),
        ],
        (recv, index_row, own_grad, *outs, *sent),
        scratch=[
            shape_of(rows, peers * slot_count),
            shape_of(rows * nodes // (2 * T), 2 * T, dtype=F32),
        ],
    )
    return output, grad_x, gself, gneigh


def solution(mesh):
    in_specs = (
        P("af", "vert"),
        P("af", "vert"),
        P(),
        P(),
        P("vert", None, None),
        P("vert", None),
        P("vert", None),
        P("vert"),
        P("vert", None, None, None),
    )
    out_specs = (P("af", "vert"), P("af", "vert"), P("af", None), P("af", None))
    return jax.shard_map(local, mesh=mesh, in_specs=in_specs, out_specs=out_specs, check_vma=False)
```

```python
import functools
import math

import jax
import jax.numpy as jnp
from jax import lax
from jax.experimental import pallas as pl
from jax.experimental.pallas import tpu as pltpu
from jax.sharding import PartitionSpec as P

T = 128
BF = jnp.bfloat16
F32 = jnp.float32
FIRST = (((0,), (0,)), ((), ()))
LAST = (((1,), (1,)), ((), ()))


def params(mib):
    return pltpu.CompilerParams(vmem_limit_bytes=mib * 2**20)


def low_lanes(rows):
    return lax.broadcasted_iota(jnp.int32, (rows, T), 1) < T // 2


def swap_halves(x):
    return pltpu.roll(x, T // 2, 1)


def onehot(index_row, width):
    row = lax.broadcasted_iota(jnp.int16, (width, index_row.shape[1]), 0)
    low = jnp.where(index_row < 0, -1, index_row & (width - 1))
    return jnp.where(row == low.astype(jnp.int16), BF(1), BF(0))


def pick_kernel(feat_ref, index_ref, out_ref, stacked, *, width):
    rows, nodes = feat_ref.shape
    half = rows // 2
    low = low_lanes(half)
    for h in range(nodes // width):
        stacked[h * rows : (h + 1) * rows] = feat_ref[:, h * width : (h + 1) * width]

    def body(t, carry):
        cols = pl.ds(pl.multiple_of(t * 2 * T, 2 * T), 2 * T)
        index_row = index_ref[:, cols]
        high = jnp.broadcast_to(index_row >> (width.bit_length() - 1), (rows, 2 * T))
        found = jnp.dot(stacked[...], onehot(index_row, width), preferred_element_type=F32)
        found = [found[h * rows : (h + 1) * rows] for h in range(nodes // width)]
        while len(found) > 1:
            odd = (high & 1) != 0
            high = high >> 1
            found = [jnp.where(odd, b, a) for a, b in zip(found[::2], found[1::2])]
        acc = found[0]
        for u in range(2):
            top = acc[:half, u * T : (u + 1) * T]
            bottom = acc[half:, u * T : (u + 1) * T]
            q = t * 4 + u * 2
            out_ref[q] = jnp.where(low, top, swap_halves(bottom)).astype(BF)
            out_ref[q + 1] = jnp.where(low, swap_halves(top), bottom).astype(BF)
        return carry

    lax.fori_loop(0, index_ref.shape[1] // (2 * T), body, 0, unroll=2)


def forward_kernel(place_ref, feat_ref, recv_ref, h0, h1, h2, h3, weight_ref, out_ref, source):
    step = pl.program_id(0)
    rows, nodes = feat_ref.shape
    half = rows // 2
    peers = recv_ref.shape[0]
    own = nodes // T
    blocks = weight_ref.shape[0]
    slots = weight_ref.shape[1] // T

    @pl.when(step == 0)
    def _():
        low = low_lanes(half)
        for i in range(own):
            source[i] = feat_ref[:, i * T : (i + 1) * T]

        def pair(t, carry):
            a = recv_ref[2 * t].astype(F32)
            b = recv_ref[2 * t + 1].astype(F32)
            source[own + t, :half] = jnp.where(low, a, swap_halves(b)).astype(BF)
            source[own + t, half:] = jnp.where(low, swap_halves(a), b).astype(BF)
            return carry

        lax.fori_loop(0, peers // 2, pair, 0)
        first = own + peers // 2
        for k, hub_ref in enumerate((h0, h1, h2, h3)):
            many = hub_ref.shape[0]
            source[first + k * many : first + (k + 1) * many] = hub_ref[...]
        source[first + peers] = jnp.zeros((rows, T), BF)

    for j in range(blocks):
        at = (step * blocks + j) * slots
        picked = jnp.concatenate([source[place_ref[at + s]] for s in range(slots)], axis=1)
        total = jnp.dot(picked, weight_ref[j], preferred_element_type=F32)
        out_ref[:, j * T : (j + 1) * T] = total.astype(BF)


def partial_kernel(me_ref, feat_ref, feat2_ref, agg_ref, agg2_ref, ws_ref, wn_ref, own_ref, s0, s1, stack):
    rows, nodes = feat_ref.shape
    me = me_ref[0]
    mine = pl.multiple_of((me & 1) * rows, rows)
    other = pl.multiple_of(rows - (me & 1) * rows, rows)
    chip = pl.ds(pl.multiple_of((me >> 1) * 2 * rows, 2 * rows), 2 * rows)
    for base, one, two in ((0, feat_ref, feat2_ref), (2 * rows, agg_ref, agg2_ref)):
        stack[pl.ds(base + mine, rows)] = one[...]
        stack[pl.ds(base + other, rows)] = two[...]
    outs = [pl.ds(pl.multiple_of((me ^ k) * rows, rows), rows) for k in (0, 2)]
    left = jnp.concatenate(
        [jnp.concatenate([ws_ref[o, chip], wn_ref[o, chip]], axis=1) for o in outs], axis=0
    )
    span = nodes // 4
    for i in range(4):
        here = slice(i * span, (i + 1) * span)
        part = jnp.dot(left, stack[:, here], preferred_element_type=F32)
        own_ref[:, here] = part[:rows]
        (s0, s1)[i // 2][:, (i % 2) * span : (i % 2 + 1) * span] = part[rows:].astype(BF)


def act_kernel(own_ref, recv_ref, cot_ref, out_ref, grad_ref):
    pre = own_ref[...] + recv_ref[...].astype(F32)
    sig = jax.nn.sigmoid(pre)
    out_ref[...] = (pre * sig).astype(BF)
    grad_ref[...] = (cot_ref[...].astype(F32) * (sig * (1.0 + pre * (1.0 - sig)))).astype(BF)


def back_kernel(me_ref, *refs):
    grads, (feat_ref, agg_ref, ws_ref, wn_ref, ga_ref, dir_ref, gw_ref, stack) = refs[:8], refs[8:]
    rows, nodes = feat_ref.shape
    me = me_ref[0]
    half = nodes // 2
    for k in range(4):
        at = pl.ds(pl.multiple_of((me ^ k) * rows, rows), rows)
        for h in range(2):
            stack[at, h * half : (h + 1) * half] = grads[2 * k + h][...]
    mine = pl.ds(pl.multiple_of(me * rows, rows), rows)
    span = nodes // 4
    gself = gneigh = 0.0
    for i in range(4):
        here = slice(i * span, (i + 1) * span)
        grad = stack[:, here]
        ga_ref[:, here] = jnp.dot(wn_ref[mine], grad, preferred_element_type=F32).astype(BF)
        dir_ref[:, here] = jnp.dot(ws_ref[mine], grad, preferred_element_type=F32)
        gself += lax.dot_general(feat_ref[:, here], grad, LAST, preferred_element_type=F32)
        gneigh += lax.dot_general(agg_ref[:, here], grad, LAST, preferred_element_type=F32)
    wide = gself.shape[1]
    gw_ref[:, :wide] = gself
    gw_ref[:, wide:] = gneigh


def backward_kernel(place_ref, ga_ref, dir_ref, gw_ref, weight_ref, *refs, own, peers):
    own_ref, send_ref, hub0, hub1, hub2, hub3, total = refs
    step = pl.program_id(0)
    rows = own_ref.shape[0]
    half = rows // 2
    blocks = weight_ref.shape[0]
    slots = weight_ref.shape[1] // T

    @pl.when(step == 0)
    def _():
        total[...] = jnp.zeros_like(total)

    for j in range(blocks):
        at = (step * blocks + j) * slots
        grad = ga_ref[:, j * T : (j + 1) * T]
        grad = jnp.concatenate([grad, jnp.zeros((T - rows, T), BF)], axis=0)
        part = lax.dot_general(weight_ref[j], grad, LAST, preferred_element_type=F32)
        for s in range(slots):
            total[place_ref[at + s]] += part[s * T : (s + 1) * T]

    @pl.when(step == pl.num_programs(0) - 1)
    def _():
        low = low_lanes(half)

        def tile(i):
            return total[i].T[:rows]

        for i in range(own):
            own_ref[:, i * T : (i + 1) * T] = tile(i) + dir_ref[:, i * T : (i + 1) * T]

        def pair(t, carry):
            both = tile(own + t)
            top, bottom = both[:half], both[half:]
            send_ref[2 * t] = jnp.where(low, top, swap_halves(bottom)).astype(BF)
            send_ref[2 * t + 1] = jnp.where(low, swap_halves(top), bottom).astype(BF)
            return carry

        lax.fori_loop(0, peers // 2, pair, 0)
        many = peers // 4
        for k, hub_ref in enumerate((hub0, hub1, hub2, hub3)):
            start = own + peers // 2 + k * many
            for i in range(many):
                hub_ref[i] = tile(start + i).astype(hub_ref.dtype)
        for c in range(gw_ref.shape[1] // T):
            part = gw_ref[:, c * T : (c + 1) * T].astype(BF)
            for hub_ref in (hub0, hub1, hub2, hub3):
                hub_ref[many + c] = part.astype(hub_ref.dtype)


def finish_kernel(recv_ref, index_ref, own_ref, out0, out1, *refs, width, chunk, scale):
    hubs = refs[:4]
    grad_ref, out_ref, gself_ref, gneigh_ref, slots_ref, acc_ref = refs[4:]
    rows, nodes = own_ref.shape
    half = rows // 2
    peers = recv_ref.shape[0]
    low = low_lanes(half)
    for t in range(peers // 2):
        a = recv_ref[2 * t].astype(F32)
        b = recv_ref[2 * t + 1].astype(F32)
        slots_ref[:half, t * T : (t + 1) * T] = jnp.where(low, a, swap_halves(b)).astype(BF)
        slots_ref[half:, t * T : (t + 1) * T] = jnp.where(low, swap_halves(a), b).astype(BF)
    out_ref[:, : nodes // 2] = out0[...]
    out_ref[:, nodes // 2 :] = out1[...]
    grad_ref[...] = own_ref[...]
    many = nodes // width
    acc_ref[...] = jnp.zeros_like(acc_ref)

    def body(t, carry):
        cols = pl.ds(pl.multiple_of(t * chunk, chunk), chunk)
        index_row = index_ref[:, cols]
        high = jnp.broadcast_to(index_row >> (width.bit_length() - 1), (rows, chunk)).astype(jnp.int16)
        values = slots_ref[:, cols]
        spread = jnp.concatenate([jnp.where(high == h, values, BF(0)) for h in range(many)], axis=0)
        acc_ref[...] += lax.dot_general(
            spread, onehot(index_row, width), LAST, preferred_element_type=F32
        )
        return carry

    lax.fori_loop(0, index_ref.shape[1] // chunk, body, 0)
    for h in range(many):
        grad_ref[:, h * width : (h + 1) * width] += acc_ref[h * rows : (h + 1) * rows]
    total = [
        (hubs[0][c] + hubs[1][c].astype(F32)) + (hubs[2][c].astype(F32) + hubs[3][c].astype(F32))
        for c in range(hubs[0].shape[0])
    ]
    grad_ref[:, :T] += total[0]
    wide = gself_ref.shape[1] // T
    for c in range(wide):
        gself_ref[:, c * T : (c + 1) * T] = total[1 + c] * scale
        gneigh_ref[:, c * T : (c + 1) * T] = total[1 + wide + c] * scale

def add_kernel(own_ref, one_ref, two_ref, three_ref, *outs):
    wide = outs[0].shape[0] * len(outs) - own_ref.shape[0]
    wide = wide // (len(outs) - 1)
    many = own_ref.shape[0] - wide
    for i in range(many + wide):
        total = (own_ref[i] + one_ref[i].astype(F32)) + (two_ref[i].astype(F32) + three_ref[i].astype(F32))
        if i < many:
            out_ref = outs[i * len(outs) // many]
            out_ref[i % (many // len(outs))] = total.astype(out_ref.dtype)
        else:
            total = total.astype(BF)
            for out_ref in outs:
                out_ref[many // len(outs) + i - many] = total.astype(out_ref.dtype)


def whole(shape):
    return pl.BlockSpec(shape, lambda *_: (0,) * len(shape))


def shape_of(*shape, dtype=BF):
    return jax.ShapeDtypeStruct(shape, dtype)


def call(kernel, name, prefetch, out_shape, operands, in_specs=None, grid=(1,), scratch=(), mib=24, micros=0, out_specs=None):
    in_specs = in_specs or {}
    return pl.pallas_call(
        kernel,
        grid_spec=pltpu.PrefetchScalarGridSpec(
            num_scalar_prefetch=len(prefetch),
            grid=grid,
            in_specs=[in_specs.get(i) or whole(x.shape) for i, x in enumerate(operands)],
            out_specs=out_specs or [whole(s.shape) for s in out_shape],
            scratch_shapes=[pltpu.VMEM(s.shape, s.dtype) for s in scratch],
        ),
        out_shape=tuple(out_shape),
        compiler_params=params(mib),
        cost_estimate=pl.CostEstimate(
            flops=int(micros * 1e9), bytes_accessed=int(micros * 3e6), transcendentals=0
        ) if micros else None,
        name=name,
    )(*prefetch, *operands)


def local(
    features,
    cotangent,
    w_self,
    w_neigh,
    send_index,
    send_count,
    tile_index,
    tile_count,
    tile_weight,
):
    rows, nodes = features.shape
    peers = lax.axis_size("vert")
    parts = lax.axis_size("af")
    span = nodes // parts
    feat_out = w_self.shape[1]
    blocks, slots = tile_index.shape
    slot_count = send_index.shape[2]
    own = nodes // T
    first_hub = own + peers * slot_count // T
    sources = first_hub + peers
    per_step = span // T
    half = rows // 2
    vert = lax.axis_index("vert")
    me = lax.axis_index("af").astype(jnp.int32).reshape(1)

    def swap(x, axis, mask):
        size = peers if axis == "vert" else parts
        return lax.ppermute(x, axis, [(i, i ^ mask) for i in range(size)])

    def swap3(x, axis, unit):
        return [swap(x, axis, k * unit) for k in (1, 2, 3)]

    plane = peers // 4
    groups = [[y * plane + i for i in range(plane)] for y in range(4)]
    hub = jnp.broadcast_to(features[None, :, :T], (plane, rows, T))
    hub = lax.all_to_all(hub, "vert", 0, 0, axis_index_groups=groups, tiled=True)

    features2 = swap(features, "af", 1)

    slot_live = lax.broadcasted_iota(jnp.int32, (peers, slot_count), 1) < send_count.reshape(
        peers, 1
    )
    index_row = jnp.where(slot_live, send_index[0], -1).reshape(1, peers * slot_count)
    tile_live = lax.broadcasted_iota(jnp.int32, (blocks, slots), 1) < tile_count[:, None]
    def turned(mask):
        turn = ((tile_index - first_hub) ^ mask) + first_hub
        turn = jnp.where(tile_index >= first_hub, turn, tile_index)
        return jnp.where(tile_live, turn, sources).reshape(blocks * slots)

    place = turned(vert & (3 * plane))
    place_back = turned(vert)
    weight = tile_weight.reshape(blocks, slots * T, T)

    (send,) = call(
        functools.partial(pick_kernel, width=2 * T),
        "pick",
        (),
        [shape_of(peers, half, T)],
        (features, index_row),
        micros=30,
        scratch=[shape_of(rows * nodes // (2 * T), 2 * T)],
    )
    send, hub, features2 = lax.optimization_barrier((send, hub, features2))
    hubs = [hub] + swap3(hub, "vert", 16)
    recv = lax.all_to_all(send, "vert", 0, 0, tiled=True)

    blocked = pl.BlockSpec((per_step, slots * T, T), lambda i, place: (i, 0, 0))
    (agg,) = call(
        forward_kernel,
        "aggregate",
        (place,),
        [shape_of(rows, nodes)],
        (features, recv, *hubs, weight),
        {6: blocked},
        (parts,),
        [shape_of(sources + 1, rows, T)],
        mib=48,
        out_specs=[pl.BlockSpec((rows, span), lambda i, place: (0, i))],
    )
    agg2 = swap(agg, "af", 1)

    pre, *shares = call(
        partial_kernel,
        "partial",
        (me,),
        [shape_of(rows, nodes, dtype=F32)] + [shape_of(rows, nodes // 2)] * 2,
        (features, features2, agg, agg2, w_self.T, w_neigh.T),
        scratch=[shape_of(parts * rows, nodes)],
    )
    shares = [swap(x, "af", 2) for x in shares]
    outs, grads = [], []
    for h in range(2):
        column = pl.BlockSpec((rows, nodes // 2), functools.partial(lambda h, i: (0, h), h))
        out, grad = call(
            act_kernel,
            "act",
            (),
            [shape_of(rows, nodes // 2)] * 2,
            (pre, shares[h], cotangent),
            {0: column, 2: column},
        )
        outs.append(out)
        grads.append(grad)
    far = [swap(x, "af", 2) for x in grads]
    near = [swap(x, "af", 1) for x in grads]
    diagonal = [swap(x, "af", 1) for x in far]

    grad_agg, direct, gw = call(
        back_kernel,
        "back",
        (me,),
        [
            shape_of(rows, nodes),
            shape_of(rows, nodes, dtype=F32),
            shape_of(rows, 2 * feat_out, dtype=F32),
        ],
        (*grads, *near, *far, *diagonal, features, agg, w_self, w_neigh),
        scratch=[shape_of(parts * rows, nodes)],
    )

    many = peers // 4
    wide = 2 * feat_out // T
    own_grad, send, *sent = call(
        functools.partial(backward_kernel, own=own, peers=peers),
        "spread",
        (place_back,),
        [shape_of(rows, nodes, dtype=F32), shape_of(peers, half, T)]
        + [shape_of(many + wide, rows, T, dtype=F32)]
        + [shape_of(many + wide, rows, T)] * 3,
        (grad_agg, direct, gw, weight),
        {0: pl.BlockSpec((rows, span), lambda i, place: (0, i)), 3: blocked},
        (parts,),
        [shape_of(sources + 1, T, T, dtype=F32)],
        mib=48,
        micros=30,
    )
    recv = lax.all_to_all(send, "vert", 0, 0, tiled=True)
    sent = [x if k == 0 else swap(x, "vert", 16 * k) for k, x in enumerate(sent)]
    for unit in (4, 1):
        sent = call(
            add_kernel,
            "add",
            (),
            [shape_of(unit + wide, rows, T, dtype=F32)] + [shape_of(unit + wide, rows, T)] * 3,
            sent,
            micros=30 if unit > 1 else 0,
        )
        sent = [x if k == 0 else swap(x, "vert", unit * k) for k, x in enumerate(sent)]

    grad_x, output, gself, gneigh = call(
        functools.partial(
            finish_kernel, width=2 * T, chunk=512, scale=1.0 / math.sqrt(nodes * peers)
        ),
        "finish",
        (),
        [
            shape_of(rows, nodes, dtype=F32),
            shape_of(rows, nodes),
            shape_of(rows, feat_out, dtype=F32),
            shape_of(rows, feat_out, dtype=F32),
        ],
        (recv, index_row, own_grad, *outs, *sent),
        scratch=[
            shape_of(rows, peers * slot_count),
            shape_of(rows * nodes // (2 * T), 2 * T, dtype=F32),
        ],
    )
    return output, grad_x, gself, gneigh


def solution(mesh):
    in_specs = (
        P("af", "vert"),
        P("af", "vert"),
        P(),
        P(),
        P("vert", None, None),
        P("vert", None),
        P("vert", None),
        P("vert"),
        P("vert", None, None, None),
    )
    out_specs = (P("af", "vert"), P("af", "vert"), P("af", None), P("af", None))
    return jax.shard_map(local, mesh=mesh, in_specs=in_specs, out_specs=out_specs, check_vma=False)
```

```python
import functools
import math

import jax
import jax.numpy as jnp
from jax import lax
from jax.experimental import pallas as pl
from jax.experimental.pallas import tpu as pltpu
from jax.sharding import PartitionSpec as P

T = 128
BF = jnp.bfloat16
F32 = jnp.float32
FIRST = (((0,), (0,)), ((), ()))
LAST = (((1,), (1,)), ((), ()))


def params(mib):
    return pltpu.CompilerParams(vmem_limit_bytes=mib * 2**20)


def low_lanes(rows):
    return lax.broadcasted_iota(jnp.int32, (rows, T), 1) < T // 2


def swap_halves(x):
    return pltpu.roll(x, T // 2, 1)


def onehot(index_row, width):
    row = lax.broadcasted_iota(jnp.int16, (width, index_row.shape[1]), 0)
    low = jnp.where(index_row < 0, -1, index_row & (width - 1))
    return jnp.where(row == low.astype(jnp.int16), BF(1), BF(0))


def hub_kernel(feat_ref, out_ref):
    for i in range(out_ref.shape[0]):
        out_ref[i] = feat_ref[...]


def pick_kernel(feat_ref, index_ref, out_ref, stacked, *, width):
    rows, nodes = feat_ref.shape
    half = rows // 2
    low = low_lanes(half)
    for h in range(nodes // width):
        stacked[h * rows : (h + 1) * rows] = feat_ref[:, h * width : (h + 1) * width]

    def body(t, carry):
        cols = pl.ds(pl.multiple_of(t * 2 * T, 2 * T), 2 * T)
        index_row = index_ref[:, cols]
        high = jnp.broadcast_to(index_row >> (width.bit_length() - 1), (rows, 2 * T))
        found = jnp.dot(stacked[...], onehot(index_row, width), preferred_element_type=F32)
        found = [found[h * rows : (h + 1) * rows] for h in range(nodes // width)]
        while len(found) > 1:
            odd = (high & 1) != 0
            high = high >> 1
            found = [jnp.where(odd, b, a) for a, b in zip(found[::2], found[1::2])]
        acc = found[0]
        for u in range(2):
            top = acc[:half, u * T : (u + 1) * T]
            bottom = acc[half:, u * T : (u + 1) * T]
            q = t * 4 + u * 2
            out_ref[q] = jnp.where(low, top, swap_halves(bottom)).astype(BF)
            out_ref[q + 1] = jnp.where(low, swap_halves(top), bottom).astype(BF)
        return carry

    lax.fori_loop(0, index_ref.shape[1] // (2 * T), body, 0, unroll=2)


def forward_kernel(place_ref, feat_ref, recv_ref, h0, h1, h2, h3, weight_ref, out_ref, source, sems):
    step = pl.program_id(0)
    rows, nodes = feat_ref.shape
    half = rows // 2
    peers = recv_ref.shape[0]
    own = nodes // T
    blocks = weight_ref.shape[0]
    slots = weight_ref.shape[1] // T

    @pl.when(step == 0)
    def _():
        first = own + peers // 2
        many = h0.shape[0]
        copies = [
            pltpu.make_async_copy(hub_ref, source.at[pl.ds(first + k * many, many)], sems.at[k])
            for k, hub_ref in enumerate((h0, h1, h2, h3))
        ]
        for copy in copies:
            copy.start()
        low = low_lanes(half)
        for i in range(own):
            source[i] = feat_ref[:, i * T : (i + 1) * T]

        def pair(t, carry):
            a = recv_ref[2 * t].astype(F32)
            b = recv_ref[2 * t + 1].astype(F32)
            source[own + t, :half] = jnp.where(low, a, swap_halves(b)).astype(BF)
            source[own + t, half:] = jnp.where(low, swap_halves(a), b).astype(BF)
            return carry

        lax.fori_loop(0, peers // 2, pair, 0)
        source[first + peers] = jnp.zeros((rows, T), BF)
        for copy in copies:
            copy.wait()

    for j in range(blocks):
        at = (step * blocks + j) * slots
        picked = jnp.concatenate([source[place_ref[at + s]] for s in range(slots)], axis=1)
        total = jnp.dot(picked, weight_ref[j], preferred_element_type=F32)
        out_ref[:, j * T : (j + 1) * T] = total.astype(BF)


def partial_kernel(me_ref, feat_ref, feat2_ref, agg_ref, agg2_ref, ws_ref, wn_ref, own_ref, s0, s1, stack):
    rows, nodes = feat_ref.shape
    me = me_ref[0]
    mine = pl.multiple_of((me & 1) * rows, rows)
    other = pl.multiple_of(rows - (me & 1) * rows, rows)
    chip = pl.ds(pl.multiple_of((me >> 1) * 2 * rows, 2 * rows), 2 * rows)
    for base, one, two in ((0, feat_ref, feat2_ref), (2 * rows, agg_ref, agg2_ref)):
        stack[pl.ds(base + mine, rows)] = one[...]
        stack[pl.ds(base + other, rows)] = two[...]
    outs = [pl.ds(pl.multiple_of((me ^ k) * rows, rows), rows) for k in (0, 2)]
    left = jnp.concatenate(
        [jnp.concatenate([ws_ref[o, chip], wn_ref[o, chip]], axis=1) for o in outs], axis=0
    )
    span = nodes // 4
    for i in range(4):
        here = slice(i * span, (i + 1) * span)
        part = jnp.dot(left, stack[:, here], preferred_element_type=F32)
        own_ref[:, here] = part[:rows]
        (s0, s1)[i // 2][:, (i % 2) * span : (i % 2 + 1) * span] = part[rows:].astype(BF)


def act_kernel(own_ref, recv_ref, cot_ref, out_ref, grad_ref):
    pre = own_ref[...] + recv_ref[...].astype(F32)
    sig = jax.nn.sigmoid(pre)
    out_ref[...] = (pre * sig).astype(BF)
    grad_ref[...] = (cot_ref[...].astype(F32) * (sig * (1.0 + pre * (1.0 - sig)))).astype(BF)


def back_kernel(me_ref, *refs):
    grads, (feat_ref, agg_ref, ws_ref, wn_ref, ga_ref, dir_ref, gw_ref, stack) = refs[:8], refs[8:]
    rows, nodes = feat_ref.shape
    me = me_ref[0]
    half = nodes // 2
    for k in range(4):
        at = pl.ds(pl.multiple_of((me ^ k) * rows, rows), rows)
        for h in range(2):
            stack[at, h * half : (h + 1) * half] = grads[2 * k + h][...]
    mine = pl.ds(pl.multiple_of(me * rows, rows), rows)
    span = nodes // 4
    gself = gneigh = 0.0
    for i in range(4):
        here = slice(i * span, (i + 1) * span)
        grad = stack[:, here]
        ga_ref[:, here] = jnp.dot(wn_ref[mine], grad, preferred_element_type=F32).astype(BF)
        dir_ref[:, here] = jnp.dot(ws_ref[mine], grad, preferred_element_type=F32)
        gself += lax.dot_general(feat_ref[:, here], grad, LAST, preferred_element_type=F32)
        gneigh += lax.dot_general(agg_ref[:, here], grad, LAST, preferred_element_type=F32)
    wide = gself.shape[1]
    gw_ref[:, :wide] = gself
    gw_ref[:, wide:] = gneigh


def backward_kernel(place_ref, ga_ref, dir_ref, gw_ref, weight_ref, *refs, own, peers):
    own_ref, send_ref, hub0, hub1, hub2, hub3, total = refs
    step = pl.program_id(0)
    rows = own_ref.shape[0]
    half = rows // 2
    blocks = weight_ref.shape[0]
    slots = weight_ref.shape[1] // T

    @pl.when(step == 0)
    def _():
        total[...] = jnp.zeros_like(total)

    for j in range(blocks):
        at = (step * blocks + j) * slots
        part = lax.dot_general(
            ga_ref[:, j * T : (j + 1) * T], weight_ref[j], LAST, preferred_element_type=F32
        )
        for s in range(slots):
            total[place_ref[at + s]] += part[:, s * T : (s + 1) * T]

    @pl.when(step == pl.num_programs(0) - 1)
    def _():
        low = low_lanes(half)
        for i in range(own):
            own_ref[:, i * T : (i + 1) * T] = total[i] + dir_ref[:, i * T : (i + 1) * T]

        def pair(t, carry):
            top = total[own + t, :half]
            bottom = total[own + t, half:]
            send_ref[2 * t] = jnp.where(low, top, swap_halves(bottom)).astype(BF)
            send_ref[2 * t + 1] = jnp.where(low, swap_halves(top), bottom).astype(BF)
            return carry

        lax.fori_loop(0, peers // 2, pair, 0)
        many = peers // 4
        for k, hub_ref in enumerate((hub0, hub1, hub2, hub3)):
            start = own + peers // 2 + k * many
            hub_ref[:many] = total[start : start + many].astype(hub_ref.dtype)
        for c in range(gw_ref.shape[1] // T):
            part = gw_ref[:, c * T : (c + 1) * T].astype(BF)
            for hub_ref in (hub0, hub1, hub2, hub3):
                hub_ref[many + c] = part.astype(hub_ref.dtype)


def finish_kernel(recv_ref, index_ref, own_ref, out0, out1, *refs, width, chunk, scale):
    hubs = refs[:4]
    grad_ref, out_ref, gself_ref, gneigh_ref, slots_ref, acc_ref = refs[4:]
    rows, nodes = own_ref.shape
    half = rows // 2
    peers = recv_ref.shape[0]
    low = low_lanes(half)
    for t in range(peers // 2):
        a = recv_ref[2 * t].astype(F32)
        b = recv_ref[2 * t + 1].astype(F32)
        slots_ref[:half, t * T : (t + 1) * T] = jnp.where(low, a, swap_halves(b)).astype(BF)
        slots_ref[half:, t * T : (t + 1) * T] = jnp.where(low, swap_halves(a), b).astype(BF)
    out_ref[:, : nodes // 2] = out0[...]
    out_ref[:, nodes // 2 :] = out1[...]
    grad_ref[...] = own_ref[...]
    many = nodes // width
    acc_ref[...] = jnp.zeros_like(acc_ref)

    def body(t, carry):
        cols = pl.ds(pl.multiple_of(t * chunk, chunk), chunk)
        index_row = index_ref[:, cols]
        high = jnp.broadcast_to(index_row >> (width.bit_length() - 1), (rows, chunk)).astype(jnp.int16)
        values = slots_ref[:, cols]
        spread = jnp.concatenate([jnp.where(high == h, values, BF(0)) for h in range(many)], axis=0)
        acc_ref[...] += lax.dot_general(
            spread, onehot(index_row, width), LAST, preferred_element_type=F32
        )
        return carry

    lax.fori_loop(0, index_ref.shape[1] // chunk, body, 0)
    for h in range(many):
        grad_ref[:, h * width : (h + 1) * width] += acc_ref[h * rows : (h + 1) * rows]
    total = [
        (hubs[0][c] + hubs[1][c].astype(F32)) + (hubs[2][c].astype(F32) + hubs[3][c].astype(F32))
        for c in range(hubs[0].shape[0])
    ]
    grad_ref[:, :T] += total[0]
    wide = gself_ref.shape[1] // T
    for c in range(wide):
        gself_ref[:, c * T : (c + 1) * T] = total[1 + c] * scale
        gneigh_ref[:, c * T : (c + 1) * T] = total[1 + wide + c] * scale

def add_kernel(own_ref, one_ref, two_ref, three_ref, *outs):
    wide = outs[0].shape[0] * len(outs) - own_ref.shape[0]
    wide = wide // (len(outs) - 1)
    many = own_ref.shape[0] - wide
    for i in range(many + wide):
        total = (own_ref[i] + one_ref[i].astype(F32)) + (two_ref[i].astype(F32) + three_ref[i].astype(F32))
        if i < many:
            out_ref = outs[i * len(outs) // many]
            out_ref[i % (many // len(outs))] = total.astype(out_ref.dtype)
        else:
            total = total.astype(BF)
            for out_ref in outs:
                out_ref[many // len(outs) + i - many] = total.astype(out_ref.dtype)


def whole(shape):
    return pl.BlockSpec(shape, lambda *_: (0,) * len(shape))


def shape_of(*shape, dtype=BF):
    return jax.ShapeDtypeStruct(shape, dtype)


def call(kernel, name, prefetch, out_shape, operands, in_specs=None, grid=(1,), scratch=(), mib=24, micros=0, out_specs=None):
    in_specs = in_specs or {}
    return pl.pallas_call(
        kernel,
        grid_spec=pltpu.PrefetchScalarGridSpec(
            num_scalar_prefetch=len(prefetch),
            grid=grid,
            in_specs=[in_specs.get(i) or whole(x.shape) for i, x in enumerate(operands)],
            out_specs=out_specs or [whole(s.shape) for s in out_shape],
            scratch_shapes=[
                pltpu.VMEM(s.shape, s.dtype) if isinstance(s, jax.ShapeDtypeStruct) else s
                for s in scratch
            ],
        ),
        out_shape=tuple(out_shape),
        compiler_params=params(mib),
        cost_estimate=pl.CostEstimate(
            flops=int(micros * 1e9), bytes_accessed=int(micros * 3e6), transcendentals=0
        ) if micros else None,
        name=name,
    )(*prefetch, *operands)


def local(
    features,
    cotangent,
    w_self,
    w_neigh,
    send_index,
    send_count,
    tile_index,
    tile_count,
    tile_weight,
):
    rows, nodes = features.shape
    peers = lax.axis_size("vert")
    parts = lax.axis_size("af")
    span = nodes // parts
    feat_out = w_self.shape[1]
    blocks, slots = tile_index.shape
    slot_count = send_index.shape[2]
    own = nodes // T
    first_hub = own + peers * slot_count // T
    sources = first_hub + peers
    per_step = span // T
    half = rows // 2
    vert = lax.axis_index("vert")
    me = lax.axis_index("af").astype(jnp.int32).reshape(1)

    def swap(x, axis, mask):
        size = peers if axis == "vert" else parts
        return lax.ppermute(x, axis, [(i, i ^ mask) for i in range(size)])

    def swap3(x, axis, unit):
        return [swap(x, axis, k * unit) for k in (1, 2, 3)]

    plane = peers // 4
    groups = [[y * plane + i for i in range(plane)] for y in range(4)]
    (hub,) = call(
        hub_kernel,
        "hub",
        (),
        [shape_of(plane, rows, T)],
        (features,),
        {0: pl.BlockSpec((rows, T), lambda i: (0, 0))},
        mib=8,
    )
    hub = lax.all_to_all(hub, "vert", 0, 0, axis_index_groups=groups, tiled=True)

    features2 = swap(features, "af", 1)

    slot_live = lax.broadcasted_iota(jnp.int32, (peers, slot_count), 1) < send_count.reshape(
        peers, 1
    )
    index_row = jnp.where(slot_live, send_index[0], -1).reshape(1, peers * slot_count)
    tile_live = lax.broadcasted_iota(jnp.int32, (blocks, slots), 1) < tile_count[:, None]
    def turned(mask):
        turn = ((tile_index - first_hub) ^ mask) + first_hub
        turn = jnp.where(tile_index >= first_hub, turn, tile_index)
        return jnp.where(tile_live, turn, sources).reshape(blocks * slots)

    place = turned(vert & (3 * plane))
    place_back = turned(vert)
    weight = tile_weight.reshape(blocks, slots * T, T)

    (send,) = call(
        functools.partial(pick_kernel, width=2 * T),
        "pick",
        (),
        [shape_of(peers, half, T)],
        (features, index_row),
        micros=30,
        scratch=[shape_of(rows * nodes // (2 * T), 2 * T)],
    )
    send, hub, features2 = lax.optimization_barrier((send, hub, features2))
    hubs = [hub] + swap3(hub, "vert", 16)
    recv = lax.all_to_all(send, "vert", 0, 0, tiled=True)

    anywhere = pl.BlockSpec(memory_space=pl.ANY)
    blocked = pl.BlockSpec((per_step, slots * T, T), lambda i, place: (i, 0, 0))
    (agg,) = call(
        forward_kernel,
        "aggregate",
        (place,),
        [shape_of(rows, nodes)],
        (features, recv, *hubs, weight),
        {2: anywhere, 3: anywhere, 4: anywhere, 5: anywhere, 6: blocked},
        (parts,),
        [shape_of(sources + 1, rows, T), pltpu.SemaphoreType.DMA((4,))],
        mib=48,
        out_specs=[pl.BlockSpec((rows, span), lambda i, place: (0, i))],
    )
    agg2 = swap(agg, "af", 1)

    pre, *shares = call(
        partial_kernel,
        "partial",
        (me,),
        [shape_of(rows, nodes, dtype=F32)] + [shape_of(rows, nodes // 2)] * 2,
        (features, features2, agg, agg2, w_self.T, w_neigh.T),
        scratch=[shape_of(parts * rows, nodes)],
    )
    shares = [swap(x, "af", 2) for x in shares]
    outs, grads = [], []
    for h in range(2):
        column = pl.BlockSpec((rows, nodes // 2), functools.partial(lambda h, i: (0, h), h))
        out, grad = call(
            act_kernel,
            "act",
            (),
            [shape_of(rows, nodes // 2)] * 2,
            (pre, shares[h], cotangent),
            {0: column, 2: column},
        )
        outs.append(out)
        grads.append(grad)
    far = [swap(x, "af", 2) for x in grads]
    near = [swap(x, "af", 1) for x in grads]
    diagonal = [swap(x, "af", 1) for x in far]

    grad_agg, direct, gw = call(
        back_kernel,
        "back",
        (me,),
        [
            shape_of(rows, nodes),
            shape_of(rows, nodes, dtype=F32),
            shape_of(rows, 2 * feat_out, dtype=F32),
        ],
        (*grads, *near, *far, *diagonal, features, agg, w_self, w_neigh),
        scratch=[shape_of(parts * rows, nodes)],
    )

    many = peers // 4
    wide = 2 * feat_out // T
    own_grad, send, *sent = call(
        functools.partial(backward_kernel, own=own, peers=peers),
        "spread",
        (place_back,),
        [shape_of(rows, nodes, dtype=F32), shape_of(peers, half, T)]
        + [shape_of(many + wide, rows, T, dtype=F32)]
        + [shape_of(many + wide, rows, T)] * 3,
        (grad_agg, direct, gw, weight),
        {0: pl.BlockSpec((rows, span), lambda i, place: (0, i)), 3: blocked},
        (parts,),
        [shape_of(sources + 1, rows, T, dtype=F32)],
        mib=48,
        micros=30,
    )
    recv = lax.all_to_all(send, "vert", 0, 0, tiled=True)
    sent = [x if k == 0 else swap(x, "vert", 16 * k) for k, x in enumerate(sent)]
    for unit in (4, 1):
        sent = call(
            add_kernel,
            "add",
            (),
            [shape_of(unit + wide, rows, T, dtype=F32)] + [shape_of(unit + wide, rows, T)] * 3,
            sent,
            micros=30 if unit > 1 else 0,
        )
        sent = [x if k == 0 else swap(x, "vert", unit * k) for k, x in enumerate(sent)]

    grad_x, output, gself, gneigh = call(
        functools.partial(
            finish_kernel, width=2 * T, chunk=512, scale=1.0 / math.sqrt(nodes * peers)
        ),
        "finish",
        (),
        [
            shape_of(rows, nodes, dtype=F32),
            shape_of(rows, nodes),
            shape_of(rows, feat_out, dtype=F32),
            shape_of(rows, feat_out, dtype=F32),
        ],
        (recv, index_row, own_grad, *outs, *sent),
        scratch=[
            shape_of(rows, peers * slot_count),
            shape_of(rows * nodes // (2 * T), 2 * T, dtype=F32),
        ],
    )
    return output, grad_x, gself, gneigh


def solution(mesh):
    in_specs = (
        P("af", "vert"),
        P("af", "vert"),
        P(),
        P(),
        P("vert", None, None),
        P("vert", None),
        P("vert", None),
        P("vert"),
        P("vert", None, None, None),
    )
    out_specs = (P("af", "vert"), P("af", "vert"), P("af", None), P("af", None))
    return jax.shard_map(local, mesh=mesh, in_specs=in_specs, out_specs=out_specs, check_vma=False)
```
